32 devices in a mesh: seq: 8 (over y, x, core), zero: 4 (over z).
Axes of the slice: x: 2, y: 2, z: 4, core: 2. Of those that a mesh axis runs over, the one named last changes fastest.
Arguments:
- tokens: bfloat16 [4096, 1024], P(('seq', 'zero')), may hold values from -18 to 18
- projection: bfloat16 [1024, 3072], P('zero'), may hold values from -0.1875 to 0.1875
- pattern: int32 [32, 8], replicated, may hold values from 0 to 31, as said below
- upstream: bfloat16 [4096, 1024], P(('seq', 'zero')), may hold values from -6 to 6
Outputs:
- attended: bfloat16 [4096, 1024], P(('seq', 'zero'))
- token_gradient: bfloat16 [4096, 1024], P(('seq', 'zero'))
- weight_gradient: float32 [1024, 3072], P('zero')
The draws below stay inside these ranges and needn't reach their ends.
Inputs may be any that keep to these rules, and one draw needn't show every extreme that they name: `pattern`: each row names 8 different key blocks, block 0 and the row's own block among them.
All inputs are finite; a program needn't handle non-finite values.
Results may differ from the reference program's by a relative error of at most 0.01.
The reference program's roundings to bfloat16 on the way count: a program that leaves them out, or rounds other values in their place, can miss the bound.
Values may be sent and summed in bfloat16 or wider, within the bound.
A program may use at most 128 MiB of HBM per device.

```python
import jax
import jax.numpy as jnp
from jax import lax

D = 1024
HEADS = 16
HEAD = 64
BLOCK = 128
NBK = 8
TOK_DEV = 128
HD = 1024
TOKENS = 4096
N_ZERO = 4


def draw_tokens(key, part):
    base_key = jax.random.fold_in(key, 11)
    spike_key = jax.random.fold_in(key, 12)
    spike_width = D // 8
    shard_count = TOKENS // TOK_DEV
    chosen = jax.random.randint(spike_key, (shard_count, 1), 0, 8)
    column_block = (jnp.arange(D) // spike_width)[None, :]
    spike_gain = jnp.where(column_block == chosen, 3.0, 1.0).astype(jnp.float32)
    spike_gain = jnp.repeat(spike_gain, TOK_DEV, axis=0)
    base_values = jnp.clip(jax.random.normal(base_key, (TOKENS, D), jnp.float32), -6.0, 6.0)
    return (base_values * spike_gain).astype(jnp.bfloat16)


def draw_pattern(key, part):
    row_total = TOKENS // BLOCK
    row_index = jnp.arange(row_total, dtype=jnp.int32)[:, None]
    column_index = jnp.arange(row_total, dtype=jnp.int32)[None, :]
    noise_bits = jax.random.randint(jax.random.fold_in(key, 21), (row_total, row_total), 0, 1 << 16, dtype=jnp.int32)
    forced = (column_index == 0) | (jnp.abs(column_index - row_index) <= 1)
    priority = jnp.where(forced, 1 << 17, noise_bits) * row_total + column_index
    picked = lax.top_k(priority, NBK)[1]
    return picked.astype(jnp.int32)


def shard_levels(stream_key, shape, split, smallest, largest):
    loudness = 1.0
    for axis_at, shards_of in split:
        steps = jax.random.uniform(jax.random.fold_in(jax.random.fold_in(stream_key, 6), axis_at), (shards_of,), jnp.float32, smallest / len(split), largest / len(split))
        loudness = loudness * jnp.repeat(jnp.exp(steps), shape[axis_at] // shards_of).reshape((-1,) + (1,) * (len(shape) - 1 - axis_at))
    return loudness


def noise(stream_key, extent, deviation, reach, shards=(), held_as=jnp.bfloat16):
    drawn = deviation * jax.random.normal(stream_key, extent, jnp.float32)
    if shards:
        drawn = drawn * shard_levels(stream_key, extent, shards, -0.22, 0.18)
    return jnp.clip(drawn, -reach, reach).astype(held_as)


def setup_inputs(seed: int = 0) -> dict:
    key_of = jax.random.split(jax.random.key(seed), 5)
    tokens = draw_tokens(jax.random.fold_in(key_of[4], 71), 0)
    projection = noise(key_of[1], (D, 3 * HD), D ** -0.5, 0.1875, ((0, 4),))
    pattern = draw_pattern(jax.random.fold_in(key_of[4], 71), 0)
    upstream = noise(key_of[3], (TOKENS, HD), 1.0, 6.0, ((0, 32),))
    return {"tokens": tokens, "projection": projection, "pattern": pattern, "upstream": upstream}


def reference(tokens, projection, pattern, upstream):
    score_scale = HEAD ** -0.5
    row_blocks = TOKENS // BLOCK
    per_shard = TOK_DEV // BLOCK
    projected = jnp.dot(tokens, projection, preferred_element_type=jnp.float32).astype(jnp.bfloat16)
    head_slabs = jnp.moveaxis(projected.reshape(row_blocks, BLOCK, 3, HEADS, HEAD), 3, 0)
    head_upstream = jnp.moveaxis(upstream.reshape(row_blocks, BLOCK, HEADS, HEAD), 2, 0)
    owners = ((jnp.arange(row_blocks) // per_shard) % N_ZERO).astype(jnp.int32)

    def group_sum(terms):
        grouped = jnp.zeros((N_ZERO, row_blocks, BLOCK, HEAD), jnp.float32).at[owners[:, None], pattern].add(terms)
        rounded = lax.optimization_barrier(grouped.astype(jnp.bfloat16)).astype(jnp.float32)
        return jnp.sum(rounded, axis=0).astype(jnp.bfloat16)

    def one_head(packed):
        head_slab, slab_upstream = packed
        queries = head_slab[:, :, 0].astype(jnp.float32)
        key_rows = head_slab[:, :, 1]
        value_rows = head_slab[:, :, 2]
        key_chosen = key_rows[pattern].reshape(row_blocks, NBK * BLOCK, HEAD).astype(jnp.float32)
        value_chosen = value_rows[pattern].reshape(row_blocks, NBK * BLOCK, HEAD).astype(jnp.float32)
        scores = jnp.einsum("rqe,rke->rqk", queries, key_chosen) * score_scale
        row_max = jnp.max(scores, axis=-1, keepdims=True)
        exponent = jnp.exp(scores - row_max)
        prob_full = exponent / jnp.sum(exponent, axis=-1, keepdims=True)
        prob_low = lax.optimization_barrier(prob_full.astype(jnp.bfloat16)).astype(jnp.float32)
        attended = jnp.einsum("rqk,rke->rqe", prob_low, value_chosen).astype(jnp.bfloat16)
        upstream_full = slab_upstream.astype(jnp.float32)
        prob_grad = jnp.einsum("rqe,rke->rqk", upstream_full, value_chosen)
        row_delta = jnp.sum(prob_full * prob_grad, axis=-1, keepdims=True)
        score_grad = lax.optimization_barrier((prob_full * (prob_grad - row_delta) * score_scale).astype(jnp.bfloat16)).astype(jnp.float32)
        query_grad = jnp.einsum("rqk,rke->rqe", score_grad, key_chosen).astype(jnp.bfloat16)
        key_terms = jnp.einsum("rqk,rqe->rke", score_grad, queries).reshape(row_blocks, NBK, BLOCK, HEAD)
        value_terms = jnp.einsum("rqk,rqe->rke", prob_low, upstream_full).reshape(row_blocks, NBK, BLOCK, HEAD)
        return attended, query_grad, group_sum(key_terms), group_sum(value_terms)

    attended_all, query_all, key_all, value_all = lax.map(one_head, (head_slabs, head_upstream))
    attended_out = jnp.moveaxis(attended_all, 0, 2).reshape(TOKENS, HD)
    stacked = jnp.stack([query_all, key_all, value_all], axis=0)
    projected_gradient = jnp.transpose(stacked, (2, 3, 0, 1, 4)).reshape(TOKENS, 3 * HD)
    token_gradient = jnp.dot(projected_gradient, projection.T, preferred_element_type=jnp.float32).astype(jnp.bfloat16)
    weight_gradient = jnp.dot(tokens.T, projected_gradient, preferred_element_type=jnp.float32)
    return attended_out, token_gradient, weight_gradient
```

```python
import functools

import jax
import jax.numpy as jnp
from jax import lax
from jax.experimental import pallas as pl
from jax.experimental.pallas import tpu as pltpu
from jax.sharding import PartitionSpec as P

HEADS = 16
HEAD = 64
BLOCK = 128
NBK = 8
MESH = pl.DeviceIdType.MESH
F32 = jnp.float32
BF16 = jnp.bfloat16
VMEM = pl.BlockSpec(memory_space=pltpu.VMEM)
SMEM = pl.BlockSpec(memory_space=pltpu.SMEM)
LIMIT = 56 * 1024 * 1024


def remote(src, dst, send, recv, where):
    return pltpu.make_async_remote_copy(
        src_ref=src, dst_ref=dst, send_sem=send, recv_sem=recv, device_id=where, device_id_type=MESH
    )


def greet(S, Z, sme, zme):
    barrier = pltpu.get_barrier_semaphore()
    for d in range(1, S):
        pl.semaphore_signal(
            barrier, inc=1, device_id=(lax.rem(sme + d, S), zme), device_id_type=MESH
        )
    for d in range(1, Z):
        pl.semaphore_signal(
            barrier, inc=1, device_id=(sme, lax.rem(zme + d, Z)), device_id_type=MESH
        )
    pl.semaphore_wait(barrier, S + Z - 2)


def gather_kernel(
    S, Z, tok_ref, w_ref, up_ref, tokg_ref, wg_ref, q_ref, kv_ref, u_ref,
    ts, tr, ws, wr, us, ur, ks, kr,
):
    sme, zme = lax.axis_index("seq"), lax.axis_index("zero")
    T = tok_ref.shape[0]
    W = w_ref.shape[1]

    def rows(i):
        return pl.ds(pl.multiple_of(i * T, T), T)

    def wrows(i):
        return pl.ds(pl.multiple_of(i * W, W), W)

    def w_copy(d, owner, peer):
        return remote(w_ref, wg_ref.at[:, wrows(owner)], ws.at[d], wr.at[d], (sme, peer))

    def t_copy(d, owner, peer):
        return remote(tok_ref, tokg_ref.at[rows(owner)], ts.at[d], tr.at[d], (peer, zme))

    def u_copy(d, owner, peer, part):
        return remote(up_ref.at[part], u_ref.at[rows(owner)], us.at[d], ur.at[d], (peer, zme))

    def k_copy(zd, d, owner, peer, block):
        at = kv_ref.at[:, owner, rows(block)]
        src = kv_ref.at[:, zme, rows(block)]
        return remote(src, at, ks.at[zd, d], kr.at[zd, d], (sme, peer))

    greet(S, Z, sme, zme)
    for d in range(1, Z):
        w_copy(d, zme, lax.rem(zme + d, Z)).start()
    for d in range(1, S):
        t_copy(d, sme, lax.rem(sme + d, S)).start()
    for d in range(1, S):
        peer = lax.rem(sme + d, S)
        u_copy(d, sme, peer, peer).start()
    wg_ref[:, wrows(zme), :] = w_ref[...]
    tokg_ref[rows(sme), :] = tok_ref[...]
    u_ref[rows(sme), :] = up_ref[sme]
    for d in range(1, Z):
        w_copy(d, lax.rem(zme + Z - d, Z), lax.rem(zme + d, Z)).wait_recv()

    def project(d):
        block = lax.rem(sme + S - d, S)
        here = tokg_ref[rows(block), :]
        q_ref[rows(block), :] = jnp.dot(here, wg_ref[0], preferred_element_type=F32).astype(BF16)
        for i in range(2):
            kv_ref[i, zme, rows(block), :] = jnp.dot(
                here, wg_ref[i + 1], preferred_element_type=F32
            ).astype(BF16)
        for zd in range(1, Z):
            k_copy(zd, d, zme, lax.rem(zme + zd, Z), block).start()

    project(0)

    def step(d, carry):
        t_copy(d, lax.rem(sme + S - d, S), lax.rem(sme + d, S)).wait_recv()
        project(d)
        return carry

    lax.fori_loop(1, S, step, 0)

    def finish(d, carry):
        block = lax.rem(sme + S - d, S)
        for zd in range(1, Z):
            copy = k_copy(zd, d, lax.rem(zme + Z - zd, Z), lax.rem(zme + zd, Z), block)
            copy.wait_recv()
            k_copy(zd, d, zme, lax.rem(zme + zd, Z), block).wait_send()
        return carry

    for d in range(1, S):
        peer = lax.rem(sme + d, S)
        u_copy(d, lax.rem(sme + S - d, S), peer, peer).wait_recv()
        u_copy(d, sme, peer, peer).wait_send()
        t_copy(d, sme, peer).wait_send()
    for d in range(1, Z):
        w_copy(d, zme, lax.rem(zme + d, Z)).wait_send()
    lax.fori_loop(0, S, finish, 0)


def attend_kernel(S, Z, per_shard, pat_ref, q_ref, kv_ref, u_ref, o_ref, dq_ref, dkv_ref, acc):
    zme = lax.axis_index("zero")
    hc = q_ref.shape[1]
    heads = hc // HEAD
    local = S * per_shard
    total = Z * local
    scale = HEAD ** (-0.5)

    def clear(i, carry):
        acc[0, i] = jnp.zeros((BLOCK, hc), F32)
        acc[1, i] = jnp.zeros((BLOCK, hc), F32)
        return carry

    lax.fori_loop(0, total, clear, 0)
    lane = lax.broadcasted_iota(jnp.int32, (BLOCK, hc), 1) // HEAD

    def split(x):
        if heads == 1:
            return x
        return jnp.concatenate([jnp.where(lane == h, x, jnp.zeros_like(x)) for h in range(heads)], axis=0)

    def join(x):
        parts = [
            x[h * HEAD : (h + 1) * HEAD, h * BLOCK : (h + 1) * BLOCK] for h in range(heads)
        ]
        both = parts[0] if heads == 1 else jnp.concatenate(parts, axis=0)
        return both.T.astype(BF16)

    def nt(a, b):
        return lax.dot_general(a, b, (((1,), (1,)), ((), ())), preferred_element_type=F32)

    def tn(a, b):
        return lax.dot_general(a, b, (((0,), (0,)), ((), ())), preferred_element_type=F32)

    def step(r, carry):
        row = (r // per_shard * Z + zme) * per_shard + r % per_shard
        slots = []
        for j in range(NBK):
            b = pat_ref[row, j]
            shard = b // per_shard
            slots.append(shard % Z * local + shard // Z * per_shard + b % per_shard)
        at = pl.ds(pl.multiple_of(r * BLOCK, BLOCK), BLOCK)
        qq = split(q_ref[at, :])
        uu = split(u_ref[at, :])
        keys = jnp.concatenate([kv_ref[0, s] for s in slots], axis=0)
        values = jnp.concatenate([kv_ref[1, s] for s in slots], axis=0)
        scores = nt(keys, qq) * scale
        top = jnp.max(scores, axis=0, keepdims=True)
        exponent = jnp.exp(scores - top)
        prob = exponent * (1.0 / jnp.sum(exponent, axis=0, keepdims=True))
        low = prob.astype(BF16)
        grad = nt(values, uu)
        delta = jnp.sum(prob * grad, axis=0, keepdims=True)
        sg = (prob * (grad - delta) * scale).astype(BF16)
        o_ref[at, :] = join(tn(values, low))
        dq_ref[at, :] = join(tn(keys, sg))
        dk = jnp.dot(sg, qq, preferred_element_type=F32)
        dv = jnp.dot(low, uu, preferred_element_type=F32)
        for j in range(NBK):
            acc[0, slots[j]] += dk[j * BLOCK : (j + 1) * BLOCK]
            acc[1, slots[j]] += dv[j * BLOCK : (j + 1) * BLOCK]
        return carry

    lax.fori_loop(0, local, step, 0)

    def store(i, carry):
        dkv_ref[0, i] = acc[0, i].astype(BF16)
        dkv_ref[1, i] = acc[1, i].astype(BF16)
        return carry

    lax.fori_loop(0, total, store, 0)


def reduce_kernel(
    S, Z, o_ref, dq_ref, dkv_ref, tokg_ref, wg_ref, att_ref, tg_ref, wo_ref,
    kbuf, grads, wacc, wsend, wbuf, town, tsend, tbuf,
    os, orr, ks, kr, ws, wr, ts, tr, gs, gr,
):
    sme, zme = lax.axis_index("seq"), lax.axis_index("zero")
    T = att_ref.shape[1]
    W = wo_ref.shape[2]

    def rows(i):
        return pl.ds(pl.multiple_of(i * T, T), T)

    def wrows(i):
        return pl.ds(pl.multiple_of(i * W, W), W)

    def speer(d):
        return lax.rem(sme + d, S)

    def sfrom(d):
        return lax.rem(sme + S - d, S)

    def zpeer(d):
        return lax.rem(zme + d, Z)

    def k_copy(d):
        return remote(dkv_ref.at[:, zpeer(d)], kbuf.at[d - 1], ks.at[d], kr.at[d], (sme, zpeer(d)))

    def o_copy(d, owner):
        return remote(
            o_ref.at[rows(speer(d))], att_ref.at[owner], os.at[d], orr.at[d], (speer(d), zme)
        )

    def w_copy(d):
        return remote(
            wsend.at[:, wrows(zpeer(d))], wbuf.at[d - 1], ws.at[d], wr.at[d], (sme, zpeer(d))
        )

    def t_copy(d):
        return remote(tsend.at[d - 1], tbuf.at[d - 1], ts.at[d], tr.at[d], (speer(d), zme))

    def g_copy(d, owner):
        return remote(wo_ref.at[sme], wo_ref.at[owner], gs.at[d], gr.at[d], (speer(d), zme))

    def weight_part(i):
        part = lax.dot_general(
            tokg_ref[...], grads[i], (((0,), (0,)), ((), ())), preferred_element_type=F32
        )
        wacc[i] = part
        wsend[i] = part.astype(BF16)

    greet(S, Z, sme, zme)
    for d in range(1, Z):
        k_copy(d).start()
    for d in range(1, S):
        o_copy(d, sme).start()
    att_ref[sme] = o_ref[rows(sme), :]
    grads[0] = dq_ref[...]
    weight_part(0)
    for d in range(1, Z):
        k_copy(d).wait_recv()
    for i in range(2):
        total = dkv_ref[i, zme].astype(F32)
        for d in range(1, Z):
            total += kbuf[d - 1, i].astype(F32)
        grads[i + 1] = total.astype(BF16)
    for i in range(2):
        weight_part(i + 1)
    for d in range(1, Z):
        w_copy(d).start()

    def token_part(block):
        total = None
        for i in range(3):
            part = lax.dot_general(
                grads[i, rows(block), :], wg_ref[i], (((1,), (1,)), ((), ())),
                preferred_element_type=F32,
            )
            total = part if total is None else total + part
        return total

    def send_tokens(d, carry):
        tsend[d - 1] = token_part(speer(d)).astype(BF16)
        t_copy(d).start()
        return carry

    lax.fori_loop(1, S, send_tokens, 0)
    town[...] = token_part(sme)
    for d in range(1, Z):
        w_copy(d).wait_recv()
    for i in range(3):
        total = wacc[i, wrows(zme), :]
        for d in range(1, Z):
            total += wbuf[d - 1, i].astype(F32)
        wo_ref[sme, i] = total.astype(BF16)
    for d in range(1, S):
        g_copy(d, sme).start()

    def add_tokens(d, carry):
        t_copy(d).wait_recv()
        town[...] += tbuf[d - 1].astype(F32)
        return carry

    lax.fori_loop(1, S, add_tokens, 0)
    tg_ref[...] = town[...].astype(BF16)
    for d in range(1, Z):
        k_copy(d).wait_send()
        w_copy(d).wait_send()
    for d in range(1, S):
        o_copy(d, sfrom(d)).wait_recv()
        o_copy(d, sme).wait_send()
        t_copy(d).wait_send()
        g_copy(d, sfrom(d)).wait_recv()
        g_copy(d, sme).wait_send()


def dma(*shape):
    return pltpu.SemaphoreType.DMA(shape)


def on_device(tokens, projection, pattern, upstream):
    S = lax.axis_size("seq")
    Z = lax.axis_size("zero")
    T, D = tokens.shape
    hc = HEADS // S * HEAD
    W = projection.shape[0]
    R = S * T
    per_shard = T // BLOCK
    total = Z * S * per_shard
    shape = jax.ShapeDtypeStruct
    own = lax.dynamic_index_in_dim(
        projection.reshape(W, 3, S, hc), lax.axis_index("seq"), axis=2, keepdims=False
    )
    own = own.transpose(1, 0, 2)
    up = upstream.reshape(T, S, hc).transpose(1, 0, 2)
    tokg, wg, q, kv, u = pl.pallas_call(
        functools.partial(gather_kernel, S, Z),
        out_shape=(
            shape((R, D), BF16), shape((3, D, hc), BF16), shape((R, hc), BF16),
            shape((2, Z, R, hc), BF16), shape((R, hc), BF16),
        ),
        in_specs=[VMEM] * 3,
        out_specs=(VMEM,) * 5,
        scratch_shapes=[
            dma(S), dma(S), dma(Z), dma(Z), dma(S), dma(S), dma(Z, S), dma(Z, S),
        ],
        compiler_params=pltpu.CompilerParams(
            collective_id=0, has_side_effects=True, vmem_limit_bytes=LIMIT
        ),
        name="gather",
    )(tokens, own, up)
    out, dq, dkv = pl.pallas_call(
        functools.partial(attend_kernel, S, Z, per_shard),
        out_shape=(
            shape((R, hc), BF16), shape((R, hc), BF16), shape((2, total, BLOCK, hc), BF16),
        ),
        in_specs=[SMEM] + [VMEM] * 3,
        out_specs=(VMEM,) * 3,
        scratch_shapes=[pltpu.VMEM((2, total, BLOCK, hc), F32)],
        compiler_params=pltpu.CompilerParams(vmem_limit_bytes=LIMIT),
        name="attend",
    )(pattern, q, kv.reshape(2, total, BLOCK, hc), u)
    att, tg, wo = pl.pallas_call(
        functools.partial(reduce_kernel, S, Z),
        out_shape=(
            shape((S, T, hc), BF16), shape((T, D), BF16), shape((S, 3, W, hc), BF16),
        ),
        in_specs=[VMEM] * 5,
        out_specs=(VMEM,) * 3,
        scratch_shapes=[
            pltpu.VMEM((Z - 1, 2, R, hc), BF16),
            pltpu.VMEM((3, R, hc), BF16),
            pltpu.VMEM((3, D, hc), F32),
            pltpu.VMEM((3, D, hc), BF16),
            pltpu.VMEM((Z - 1, 3, W, hc), BF16),
            pltpu.VMEM((T, D), F32),
            pltpu.VMEM((S - 1, T, D), BF16),
            pltpu.VMEM((S - 1, T, D), BF16),
            dma(S), dma(S), dma(Z), dma(Z), dma(Z), dma(Z), dma(S), dma(S), dma(S), dma(S),
        ],
        compiler_params=pltpu.CompilerParams(
            collective_id=1, has_side_effects=True, vmem_limit_bytes=LIMIT
        ),
        name="reduce",
    )(out, dq, dkv.reshape(2, Z, R, hc), tokg, wg)
    attended = att.transpose(1, 0, 2).reshape(T, S * hc)
    weight_gradient = wo.transpose(2, 1, 0, 3).reshape(W, 3 * S * hc).astype(F32)
    return (attended, tg, weight_gradient)


def solution(mesh):
    return jax.shard_map(
        on_device,
        mesh=mesh,
        in_specs=(P(("seq", "zero"), None), P("zero", None), P(), P(("seq", "zero"), None)),
        out_specs=(P(("seq", "zero"), None), P(("seq", "zero"), None), P("zero", None)),
        check_vma=False,
    )
```

```python
import functools

import jax
import jax.numpy as jnp
from jax import lax
from jax.experimental import pallas as pl
from jax.experimental.pallas import tpu as pltpu
from jax.sharding import PartitionSpec as P

HEADS = 16
HEAD = 64
BLOCK = 128
NBK = 8
LANES = 128
MESH = pl.DeviceIdType.MESH
F32 = jnp.float32
BF16 = jnp.bfloat16
VMEM = pl.BlockSpec(memory_space=pltpu.VMEM)
SMEM = pl.BlockSpec(memory_space=pltpu.SMEM)
LIMIT = 56 * 1024 * 1024


def remote(src, dst, send, recv, where):
    return pltpu.make_async_remote_copy(
        src_ref=src, dst_ref=dst, send_sem=send, recv_sem=recv, device_id=where, device_id_type=MESH
    )


def greet(S, Z, sme, zme):
    barrier = pltpu.get_barrier_semaphore()
    for d in range(1, S):
        pl.semaphore_signal(
            barrier, inc=1, device_id=(lax.rem(sme + d, S), zme), device_id_type=MESH
        )
    for d in range(1, Z):
        pl.semaphore_signal(
            barrier, inc=1, device_id=(sme, lax.rem(zme + d, Z)), device_id_type=MESH
        )
    pl.semaphore_wait(barrier, S + Z - 2)


def turn(x):
    return pltpu.roll(x.astype(F32), HEAD, 1).astype(BF16)


def first_half(shape):
    return lax.broadcasted_iota(jnp.int32, shape, 1) < HEAD


def gather_kernel(
    S, Z, H, tok_ref, w_ref, up_ref, tokg_ref, wg_ref, kv_ref, qu_ref,
    wown, kvown, quown, ubuf, ts, tr, ws, wr, us, ur, ks, kr, qs, qr,
):
    sme, zme = lax.axis_index("seq"), lax.axis_index("zero")
    hme = lax.rem(zme, H)
    mate = zme + 1 - 2 * hme
    T = tok_ref.shape[0]
    W = wown.shape[1]

    def rows(i):
        return pl.ds(pl.multiple_of(i * T, T), T)

    def wrows(i):
        return pl.ds(pl.multiple_of(i * W, W), W)

    def w_copy(d, owner, peer):
        return remote(wown, wg_ref.at[:, wrows(owner)], ws.at[d], wr.at[d], (sme, peer))

    def t_copy(d, owner, peer):
        return remote(tok_ref, tokg_ref.at[rows(owner)], ts.at[d], tr.at[d], (peer, zme))

    def u_copy(d, owner, peer):
        return remote(up_ref.at[peer], ubuf.at[rows(owner)], us.at[d], ur.at[d], (peer, zme))

    def k_copy(zd, d, owner, peer, block):
        src = kvown.at[lax.rem(peer, H), rows(block)]
        return remote(src, kv_ref.at[owner, rows(block)], ks.at[zd, d], kr.at[zd, d], (sme, peer))

    def q_copy(d, group, block):
        src = quown.at[1 - hme, rows(block)]
        return remote(src, qu_ref.at[group, rows(block)], qs.at[d], qr.at[d], (sme, mate))

    if H == 2:
        half = first_half((W, LANES))
        turned = turn(w_ref[2])
        wown[0] = w_ref[0]
        wown[1] = jnp.where(half, w_ref[1], turned)
        wown[2] = jnp.where(half, turned, w_ref[1])
    else:
        wown[...] = w_ref[...]
    greet(S, Z, sme, zme)
    for d in range(1, Z):
        w_copy(d, zme, lax.rem(zme + d, Z)).start()
    for d in range(1, S):
        peer = lax.rem(sme + d, S)
        t_copy(d, sme, peer).start()
        u_copy(d, sme, peer).start()
    wg_ref[:, wrows(zme), :] = wown[...]
    tokg_ref[rows(sme), :] = tok_ref[...]
    ubuf[rows(sme), :] = up_ref[sme]
    for d in range(1, Z):
        w_copy(d, lax.rem(zme + Z - d, Z), lax.rem(zme + d, Z)).wait_recv()

    def project(d):
        block = lax.rem(sme + S - d, S)
        here = tokg_ref[rows(block), :]
        for h in range(H):
            kvown[h, rows(block), :] = jnp.dot(
                here, wg_ref[h + 1], preferred_element_type=F32
            ).astype(BF16)
        for zd in range(1, Z):
            k_copy(zd, d, zme, lax.rem(zme + zd, Z), block).start()
        kv_ref[zme, rows(block), :] = kvown[hme, rows(block), :]
        queries = jnp.dot(here, wg_ref[0], preferred_element_type=F32).astype(BF16)
        half = first_half((T, LANES))
        if H == 2:
            ups = turn(ubuf[rows(block), :])
            quown[0, rows(block), :] = jnp.where(half, queries, ups)
            quown[1, rows(block), :] = jnp.where(half, ups, queries)
            q_copy(d, hme, block).start()
        else:
            quown[0, rows(block), :] = jnp.where(half, queries, ubuf[rows(block), :])
        qu_ref[hme, rows(block), :] = quown[hme, rows(block), :]

    project(0)

    def step(d, carry):
        owner, peer = lax.rem(sme + S - d, S), lax.rem(sme + d, S)
        t_copy(d, owner, peer).wait_recv()
        u_copy(d, owner, peer).wait_recv()
        project(d)
        return carry

    lax.fori_loop(1, S, step, 0)

    def finish(d, carry):
        block = lax.rem(sme + S - d, S)
        for zd in range(1, Z):
            peer = lax.rem(zme + zd, Z)
            k_copy(zd, d, lax.rem(zme + Z - zd, Z), peer, block).wait_recv()
            k_copy(zd, d, zme, peer, block).wait_send()
        if H == 2:
            q_copy(d, 1 - hme, block).wait_recv()
            q_copy(d, hme, block).wait_send()
        return carry

    for d in range(1, S):
        peer = lax.rem(sme + d, S)
        u_copy(d, sme, peer).wait_send()
        t_copy(d, sme, peer).wait_send()
    for d in range(1, Z):
        w_copy(d, zme, lax.rem(zme + d, Z)).wait_send()
    lax.fori_loop(0, S, finish, 0)


def attend_kernel(S, Z, H, per_shard, pat_ref, qu_ref, kv_ref, do_ref, dkv_ref, acc):
    zme = lax.axis_index("zero")
    hme = zme % H
    local = S * per_shard
    total = Z * local
    scale = HEAD ** (-0.5)

    def clear(i, carry):
        acc[i] = jnp.zeros((BLOCK, LANES), F32)
        return carry

    lax.fori_loop(0, total, clear, 0)
    is_q = lax.broadcasted_iota(jnp.int32, (BLOCK, LANES), 1) // HEAD == hme
    is_dq = lax.broadcasted_iota(jnp.int32, (LANES, BLOCK), 0) // HEAD == hme

    def step(i, carry):
        r = i % local
        row = (r // per_shard * Z + zme - hme + i // local) * per_shard + r % per_shard
        slots = []
        for j in range(NBK):
            b = pat_ref[row, j]
            shard = b // per_shard
            slots.append(shard % Z * local + shard // Z * per_shard + b % per_shard)
        qu = qu_ref[i]
        none = jnp.zeros_like(qu)
        both = jnp.concatenate([jnp.where(is_q, qu, none), jnp.where(is_q, none, qu)], axis=0)
        keys = jnp.concatenate([kv_ref[s] for s in slots], axis=0)
        mixed = lax.dot_general(keys, both, (((1,), (1,)), ((), ())), preferred_element_type=F32)
        scores = mixed[:, :BLOCK] * scale
        grad = mixed[:, BLOCK:]
        top = jnp.max(scores, axis=0, keepdims=True)
        exponent = jnp.exp(scores - top)
        prob = exponent * (1.0 / jnp.sum(exponent, axis=0, keepdims=True))
        delta = jnp.sum(prob * grad, axis=0, keepdims=True)
        sg = (prob * (grad - delta) * scale).astype(BF16)
        pair = jnp.concatenate([sg, prob.astype(BF16)], axis=1)
        outs = lax.dot_general(keys, pair, (((0,), (0,)), ((), ())), preferred_element_type=F32)
        do_ref[i] = jnp.where(is_dq, outs[:, :BLOCK], outs[:, BLOCK:]).T.astype(BF16)
        terms = jnp.dot(pair, both, preferred_element_type=F32)
        for j in range(NBK):
            acc[slots[j]] += terms[j * BLOCK : (j + 1) * BLOCK]
        return carry

    lax.fori_loop(0, H * local, step, 0)

    def store(i, carry):
        dkv_ref[i] = acc[i].astype(BF16)
        return carry

    lax.fori_loop(0, total, store, 0)


def reduce_kernel(
    S, Z, H, do_ref, dkv_ref, tokg_ref, wg_ref, att_ref, tg_ref, wo_ref,
    dbuf, osend, kbuf, grads, wacc, wsend, wbuf, town, tsend, tbuf,
    ds, dr, os, orr, ks, kr, ws, wr, ts, tr, gs, gr,
):
    sme, zme = lax.axis_index("seq"), lax.axis_index("zero")
    hme = lax.rem(zme, H)
    mate = zme + 1 - 2 * hme
    T = att_ref.shape[1]
    W = wo_ref.shape[2]
    R = S * T

    def rows(i):
        return pl.ds(pl.multiple_of(i * T, T), T)

    def wrows(i):
        return pl.ds(pl.multiple_of(i * W, W), W)

    def speer(d):
        return lax.rem(sme + d, S)

    def sfrom(d):
        return lax.rem(sme + S - d, S)

    def zpeer(d):
        return lax.rem(zme + d, Z)

    def d_copy():
        return remote(do_ref.at[1 - hme], dbuf, ds, dr, (sme, mate))

    def k_copy(d):
        return remote(dkv_ref.at[zpeer(d)], kbuf.at[d - 1], ks.at[d], kr.at[d], (sme, zpeer(d)))

    def o_copy(d, owner):
        return remote(
            osend.at[rows(speer(d))], att_ref.at[owner], os.at[d], orr.at[d], (speer(d), zme)
        )

    def w_copy(d):
        return remote(
            wsend.at[:, wrows(zpeer(d))], wbuf.at[d - 1], ws.at[d], wr.at[d], (sme, zpeer(d))
        )

    def t_copy(d):
        return remote(tsend.at[d - 1], tbuf.at[d - 1], ts.at[d], tr.at[d], (speer(d), zme))

    def g_copy(d, owner):
        return remote(wo_ref.at[sme], wo_ref.at[owner], gs.at[d], gr.at[d], (speer(d), zme))

    def weight_part(i):
        part = lax.dot_general(
            tokg_ref[...], grads[i], (((0,), (0,)), ((), ())), preferred_element_type=F32
        )
        wacc[i] = part
        wsend[i] = part.astype(BF16)

    greet(S, Z, sme, zme)
    if H == 2:
        d_copy().start()
    for d in range(1, Z):
        k_copy(d).start()
    half = first_half((R, LANES))
    own = do_ref[hme]
    if H == 2:
        d_copy().wait_recv()
        other = dbuf[...]
        even = jnp.where(hme == 0, own, other)
        odd = jnp.where(hme == 0, other, own)
        grads[0] = jnp.where(half, even, odd)
        osend[...] = turn(jnp.where(half, odd, even))
    else:
        grads[0] = jnp.where(half, own, jnp.zeros_like(own))
        osend[...] = own
    for d in range(1, S):
        o_copy(d, sme).start()
    att_ref[sme] = osend[rows(sme), :]
    weight_part(0)
    for d in range(1, Z):
        k_copy(d).wait_recv()
    for h in range(H):
        total = dkv_ref[zme].astype(F32) if h == 0 else None
        for d in range(1, Z):
            if d % H == h:
                term = kbuf[d - 1].astype(F32)
                total = term if total is None else total + term
        grads[1 + lax.rem(hme + h, H)] = total.astype(BF16)
    for h in range(H):
        weight_part(1 + h)
    for d in range(1, Z):
        w_copy(d).start()

    def token_part(block):
        total = None
        for i in range(1 + H):
            part = lax.dot_general(
                grads[i, rows(block), :], wg_ref[i], (((1,), (1,)), ((), ())),
                preferred_element_type=F32,
            )
            total = part if total is None else total + part
        return total

    def send_tokens(d, carry):
        tsend[d - 1] = token_part(speer(d)).astype(BF16)
        t_copy(d).start()
        return carry

    lax.fori_loop(1, S, send_tokens, 0)
    town[...] = token_part(sme)
    for d in range(1, Z):
        w_copy(d).wait_recv()
    sums = []
    for i in range(1 + H):
        total = wacc[i, wrows(zme), :]
        for d in range(1, Z):
            total += wbuf[d - 1, i].astype(F32)
        sums.append(total)
    if H == 2:
        cut = first_half((W, LANES))
        value = pltpu.roll(jnp.where(cut, sums[2], sums[1]), HEAD, 1)
        sums = [sums[0], jnp.where(cut, sums[1], sums[2]), value]
    for i in range(1 + H):
        wo_ref[sme, i] = sums[i].astype(BF16)
    for d in range(1, S):
        g_copy(d, sme).start()

    def add_tokens(d, carry):
        t_copy(d).wait_recv()
        town[...] += tbuf[d - 1].astype(F32)
        return carry

    lax.fori_loop(1, S, add_tokens, 0)
    tg_ref[...] = town[...].astype(BF16)
    if H == 2:
        d_copy().wait_send()
    for d in range(1, Z):
        k_copy(d).wait_send()
        w_copy(d).wait_send()
    for d in range(1, S):
        o_copy(d, sfrom(d)).wait_recv()
        o_copy(d, sme).wait_send()
        t_copy(d).wait_send()
        g_copy(d, sfrom(d)).wait_recv()
        g_copy(d, sme).wait_send()


def dma(*shape):
    return pltpu.SemaphoreType.DMA(shape)


def on_device(tokens, projection, pattern, upstream):
    S = lax.axis_size("seq")
    Z = lax.axis_size("zero")
    T, D = tokens.shape
    hc = HEADS // S * HEAD
    W = projection.shape[0]
    R = S * T
    per_shard = T // BLOCK
    H = hc // HEAD
    total = Z * S * per_shard
    shape = jax.ShapeDtypeStruct
    own = lax.dynamic_index_in_dim(
        projection.reshape(W, 3, S, hc), lax.axis_index("seq"), axis=2, keepdims=False
    )
    own = own.transpose(1, 0, 2)
    up = upstream.reshape(T, S, hc).transpose(1, 0, 2)
    if H == 1:
        own = jnp.stack(
            [
                jnp.concatenate([own[0], jnp.zeros_like(own[0])], axis=1),
                jnp.concatenate([own[1], own[2]], axis=1),
            ]
        )
        up = jnp.concatenate([jnp.zeros_like(up), up], axis=2)
    tokg, wg, kv, qu = pl.pallas_call(
        functools.partial(gather_kernel, S, Z, H),
        out_shape=(
            shape((R, D), BF16), shape((1 + H, D, LANES), BF16),
            shape((Z, R, LANES), BF16), shape((H, R, LANES), BF16),
        ),
        in_specs=[VMEM] * 3,
        out_specs=(VMEM,) * 4,
        scratch_shapes=[
            pltpu.VMEM((1 + H, W, LANES), BF16),
            pltpu.VMEM((H, R, LANES), BF16),
            pltpu.VMEM((H, R, LANES), BF16),
            pltpu.VMEM((R, LANES), BF16),
            dma(S), dma(S), dma(Z), dma(Z), dma(S), dma(S), dma(Z, S), dma(Z, S), dma(S), dma(S),
        ],
        compiler_params=pltpu.CompilerParams(
            collective_id=0, has_side_effects=True, vmem_limit_bytes=LIMIT
        ),
        name="gather",
    )(tokens, own, up)
    do, dkv = pl.pallas_call(
        functools.partial(attend_kernel, S, Z, H, per_shard),
        out_shape=(
            shape((H * S * per_shard, BLOCK, LANES), BF16), shape((total, BLOCK, LANES), BF16),
        ),
        in_specs=[SMEM] + [VMEM] * 2,
        out_specs=(VMEM,) * 2,
        scratch_shapes=[pltpu.VMEM((total, BLOCK, LANES), F32)],
        compiler_params=pltpu.CompilerParams(vmem_limit_bytes=LIMIT),
        name="attend",
    )(
        pattern,
        qu.reshape(H * S * per_shard, BLOCK, LANES),
        kv.reshape(total, BLOCK, LANES),
    )
    att, tg, wo = pl.pallas_call(
        functools.partial(reduce_kernel, S, Z, H),
        out_shape=(
            shape((S, T, LANES), BF16), shape((T, D), BF16), shape((S, 1 + H, W, LANES), BF16),
        ),
        in_specs=[VMEM] * 4,
        out_specs=(VMEM,) * 3,
        scratch_shapes=[
            pltpu.VMEM((R, LANES), BF16),
            pltpu.VMEM((R, LANES), BF16),
            pltpu.VMEM((Z - 1, R, LANES), BF16),
            pltpu.VMEM((1 + H, R, LANES), BF16),
            pltpu.VMEM((1 + H, D, LANES), F32),
            pltpu.VMEM((1 + H, D, LANES), BF16),
            pltpu.VMEM((Z - 1, 1 + H, W, LANES), BF16),
            pltpu.VMEM((T, D), F32),
            pltpu.VMEM((S - 1, T, D), BF16),
            pltpu.VMEM((S - 1, T, D), BF16),
            pltpu.SemaphoreType.DMA, pltpu.SemaphoreType.DMA,
            dma(S), dma(S), dma(Z), dma(Z), dma(Z), dma(Z), dma(S), dma(S), dma(S), dma(S),
        ],
        compiler_params=pltpu.CompilerParams(
            collective_id=1, has_side_effects=True, vmem_limit_bytes=LIMIT
        ),
        name="reduce",
    )(do.reshape(H, R, LANES), dkv.reshape(Z, R, LANES), tokg, wg)
    if H == 1:
        att = att[:, :, HEAD:]
        wo = jnp.stack([wo[:, 0, :, :HEAD], wo[:, 1, :, :HEAD], wo[:, 1, :, HEAD:]], axis=1)
    attended = att.transpose(1, 0, 2).reshape(T, S * hc)
    weight_gradient = wo.transpose(2, 1, 0, 3).reshape(W, 3 * S * hc).astype(F32)
    return (attended, tg, weight_gradient)


def solution(mesh):
    return jax.shard_map(
        on_device,
        mesh=mesh,
        in_specs=(P(("seq", "zero"), None), P("zero", None), P(), P(("seq", "zero"), None)),
        out_specs=(P(("seq", "zero"), None), P(("seq", "zero"), None), P("zero", None)),
        check_vma=False,
    )
```

```python
import functools

import jax
import jax.numpy as jnp
from jax import lax
from jax.experimental import pallas as pl
from jax.experimental.pallas import tpu as pltpu
from jax.sharding import PartitionSpec as P

HEADS = 16
HEAD = 64
BLOCK = 128
NBK = 8
LANES = 128
MESH = pl.DeviceIdType.MESH
F32 = jnp.float32
BF16 = jnp.bfloat16
VMEM = pl.BlockSpec(memory_space=pltpu.VMEM)
SMEM = pl.BlockSpec(memory_space=pltpu.SMEM)
LIMIT = 56 * 1024 * 1024


def remote(src, dst, send, recv, where):
    return pltpu.make_async_remote_copy(
        src_ref=src, dst_ref=dst, send_sem=send, recv_sem=recv, device_id=where, device_id_type=MESH
    )


def greet(S, Z, sme, zme):
    barrier = pltpu.get_barrier_semaphore()
    for d in range(1, S):
        pl.semaphore_signal(
            barrier, inc=1, device_id=(lax.rem(sme + d, S), zme), device_id_type=MESH
        )
    for d in range(1, Z):
        pl.semaphore_signal(
            barrier, inc=1, device_id=(sme, lax.rem(zme + d, Z)), device_id_type=MESH
        )
    pl.semaphore_wait(barrier, S + Z - 2)


def turn(x):
    return pltpu.roll(x.astype(F32), HEAD, 1).astype(BF16)


def first_half(shape):
    return lax.broadcasted_iota(jnp.int32, shape, 1) < HEAD


def gather_kernel(
    S, Z, H, tok_ref, w_ref, up_ref, tokg_ref, wg_ref, kv_ref, qu_ref,
    wraw, wsem, wown, kvown, quown, ubuf, ts, tr, ws, wr, us, ur, ks, kr, qs, qr,
):
    sme, zme = lax.axis_index("seq"), lax.axis_index("zero")
    hme = lax.rem(zme, H)
    mate = zme + 1 - 2 * hme
    T = tok_ref.shape[0]
    W = wown.shape[1]

    def rows(i):
        return pl.ds(pl.multiple_of(i * T, T), T)

    def wrows(i):
        return pl.ds(pl.multiple_of(i * W, W), W)

    def up_part(peer):
        if H == 1:
            return up_ref.at[peer]
        return up_ref.at[:, pl.ds(pl.multiple_of(peer * LANES, LANES), LANES)]

    def raw_copy(i):
        at = pl.ds(pl.multiple_of((i * S + sme) * LANES, LANES), LANES)
        return pltpu.make_async_copy(w_ref.at[:, at], wraw.at[i], wsem.at[i])

    def w_copy(d, owner, peer):
        return remote(wown, wg_ref.at[:, wrows(owner)], ws.at[d], wr.at[d], (sme, peer))

    def t_copy(d, owner, peer):
        return remote(tok_ref, tokg_ref.at[rows(owner)], ts.at[d], tr.at[d], (peer, zme))

    def u_copy(d, owner, peer):
        return remote(up_part(peer), ubuf.at[rows(owner)], us.at[d], ur.at[d], (peer, zme))

    def k_copy(zd, d, owner, peer, block):
        src = kvown.at[lax.rem(peer, H), rows(block)]
        return remote(src, kv_ref.at[owner, rows(block)], ks.at[zd, d], kr.at[zd, d], (sme, peer))

    def q_copy(d, group, block):
        src = quown.at[1 - hme, rows(block)]
        return remote(src, qu_ref.at[group, rows(block)], qs.at[d], qr.at[d], (sme, mate))

    if H == 2:
        for i in range(3):
            raw_copy(i).start()
        for i in range(3):
            raw_copy(i).wait()
        half = first_half((W, LANES))
        turned = turn(wraw[2])
        wown[0] = wraw[0]
        wown[1] = jnp.where(half, wraw[1], turned)
        wown[2] = jnp.where(half, turned, wraw[1])
    else:
        wown[...] = w_ref[...]
    greet(S, Z, sme, zme)
    for d in range(1, Z):
        w_copy(d, zme, lax.rem(zme + d, Z)).start()
    for d in range(1, S):
        peer = lax.rem(sme + d, S)
        t_copy(d, sme, peer).start()
        u_copy(d, sme, peer).start()
    wg_ref[:, wrows(zme), :] = wown[...]
    tokg_ref[rows(sme), :] = tok_ref[...]
    if H == 1:
        ubuf[rows(sme), :] = up_ref[sme]
    else:
        ubuf[rows(sme), :] = up_ref[:, pl.ds(pl.multiple_of(sme * LANES, LANES), LANES)]
    for d in range(1, Z):
        w_copy(d, lax.rem(zme + Z - d, Z), lax.rem(zme + d, Z)).wait_recv()

    def project(d):
        block = lax.rem(sme + S - d, S)
        here = tokg_ref[rows(block), :]
        for h in range(H):
            kvown[h, rows(block), :] = jnp.dot(
                here, wg_ref[h + 1], preferred_element_type=F32
            ).astype(BF16)
        for zd in range(1, Z):
            k_copy(zd, d, zme, lax.rem(zme + zd, Z), block).start()
        kv_ref[zme, rows(block), :] = kvown[hme, rows(block), :]
        queries = jnp.dot(here, wg_ref[0], preferred_element_type=F32).astype(BF16)
        half = first_half((T, LANES))
        if H == 2:
            ups = turn(ubuf[rows(block), :])
            quown[0, rows(block), :] = jnp.where(half, queries, ups)
            quown[1, rows(block), :] = jnp.where(half, ups, queries)
            q_copy(d, hme, block).start()
        else:
            quown[0, rows(block), :] = jnp.where(half, queries, ubuf[rows(block), :])
        qu_ref[hme, rows(block), :] = quown[hme, rows(block), :]

    project(0)

    def step(d, carry):
        owner, peer = lax.rem(sme + S - d, S), lax.rem(sme + d, S)
        t_copy(d, owner, peer).wait_recv()
        u_copy(d, owner, peer).wait_recv()
        project(d)
        return carry

    lax.fori_loop(1, S, step, 0)

    def finish(d, carry):
        block = lax.rem(sme + S - d, S)
        for zd in range(1, Z):
            peer = lax.rem(zme + zd, Z)
            k_copy(zd, d, lax.rem(zme + Z - zd, Z), peer, block).wait_recv()
            k_copy(zd, d, zme, peer, block).wait_send()
        if H == 2:
            q_copy(d, 1 - hme, block).wait_recv()
            q_copy(d, hme, block).wait_send()
        return carry

    for d in range(1, S):
        peer = lax.rem(sme + d, S)
        u_copy(d, sme, peer).wait_send()
        t_copy(d, sme, peer).wait_send()
    for d in range(1, Z):
        w_copy(d, zme, lax.rem(zme + d, Z)).wait_send()
    lax.fori_loop(0, S, finish, 0)


def attend_kernel(S, Z, H, per_shard, pat_ref, qu_ref, kv_ref, do_ref, dkv_ref, acc):
    zme = lax.axis_index("zero")
    hme = zme % H
    local = S * per_shard
    total = Z * local
    scale = HEAD ** (-0.5)

    def clear(i, carry):
        acc[i] = jnp.zeros((BLOCK, LANES), F32)
        return carry

    lax.fori_loop(0, total, clear, 0)
    is_q = lax.broadcasted_iota(jnp.int32, (BLOCK, LANES), 1) // HEAD == hme
    is_dq = lax.broadcasted_iota(jnp.int32, (LANES, BLOCK), 0) // HEAD == hme

    def step(i, carry):
        r = i % local
        row = (r // per_shard * Z + zme - hme + i // local) * per_shard + r % per_shard
        slots = []
        for j in range(NBK):
            b = pat_ref[row, j]
            shard = b // per_shard
            slots.append(shard % Z * local + shard // Z * per_shard + b % per_shard)
        qu = qu_ref[i]
        none = jnp.zeros_like(qu)
        both = jnp.concatenate([jnp.where(is_q, qu, none), jnp.where(is_q, none, qu)], axis=0)
        keys = jnp.concatenate([kv_ref[s] for s in slots], axis=0)
        mixed = lax.dot_general(keys, both, (((1,), (1,)), ((), ())), preferred_element_type=F32)
        scores = mixed[:, :BLOCK] * scale
        grad = mixed[:, BLOCK:]
        top = jnp.max(scores, axis=0, keepdims=True)
        exponent = jnp.exp(scores - top)
        prob = exponent * (1.0 / jnp.sum(exponent, axis=0, keepdims=True))
        delta = jnp.sum(prob * grad, axis=0, keepdims=True)
        sg = (prob * (grad - delta) * scale).astype(BF16)
        pair = jnp.concatenate([sg, prob.astype(BF16)], axis=1)
        outs = lax.dot_general(keys, pair, (((0,), (0,)), ((), ())), preferred_element_type=F32)
        do_ref[i] = jnp.where(is_dq, outs[:, :BLOCK], outs[:, BLOCK:]).T.astype(BF16)
        terms = jnp.dot(pair, both, preferred_element_type=F32)
        for j in range(NBK):
            acc[slots[j]] += terms[j * BLOCK : (j + 1) * BLOCK]
        return carry

    lax.fori_loop(0, H * local, step, 0)

    def store(i, carry):
        dkv_ref[i] = acc[i].astype(BF16)
        return carry

    lax.fori_loop(0, total, store, 0)


def reduce_kernel(
    S, Z, H, do_ref, dkv_ref, tokg_ref, wg_ref, att_ref, tg_ref, wout_ref,
    dbuf, osend, kbuf, grads, wacc, wsend, wbuf, wo, att, part, csend, cbuf, tsend, tbuf,
    ds, dr, os, orr, ks, kr, ws, wr, cs, cr, ts, tr, gs, gr, fs, fr,
):
    sme, zme = lax.axis_index("seq"), lax.axis_index("zero")
    hme = lax.rem(zme, H)
    mate = zme + 1 - 2 * hme
    C = S // 2
    core = lax.rem(sme, 2)
    chip = sme // 2
    twin = sme + 1 - 2 * core
    T = tg_ref.shape[0]
    W = wo.shape[2]
    R = S * T
    hc = H * HEAD

    def rows(i):
        return pl.ds(pl.multiple_of(i * T, T), T)

    def wrows(i):
        return pl.ds(pl.multiple_of(i * W, W), W)

    def speer(d):
        return lax.rem(sme + d, S)

    def sfrom(d):
        return lax.rem(sme + S - d, S)

    def zpeer(d):
        return lax.rem(zme + d, Z)

    def d_copy():
        return remote(do_ref.at[1 - hme], dbuf, ds, dr, (sme, mate))

    def k_copy(d):
        return remote(dkv_ref.at[zpeer(d)], kbuf.at[d - 1], ks.at[d], kr.at[d], (sme, zpeer(d)))

    def there(d):
        return lax.rem(chip + d, C)

    def back(d):
        return lax.rem(chip + C - d, C)

    def o_copy(d, owner):
        return remote(
            osend.at[rows(speer(d))], att.at[owner], os.at[d], orr.at[d], (speer(d), zme)
        )

    def w_copy(d, i):
        return remote(
            wsend.at[i, wrows(zpeer(d))], wbuf.at[d - 1, i], ws.at[d, i], wr.at[d, i],
            (sme, zpeer(d)),
        )

    def c_copy(d):
        return remote(csend.at[d], cbuf.at[d], cs.at[d], cr.at[d], (twin, zme))

    def t_copy(d):
        return remote(
            tsend.at[d - 1], tbuf.at[d - 1], ts.at[d], tr.at[d], (there(d) * 2 + core, zme)
        )

    def span(k):
        return pl.ds(0, 1) if k == 0 else pl.ds(1, wo.shape[1] - 1)

    def g_copy(k, d, owner):
        block = wo.at[sme, span(k)]
        return remote(
            block, wo.at[owner, span(k)], gs.at[k, d], gr.at[k, d], (there(d) * 2 + core, zme)
        )

    def f_copy(k, d, side):
        block = wo.at[back(d) * 2 + core, span(k)]
        return remote(
            block, wo.at[back(d) * 2 + side, span(k)], fs.at[k, d], fr.at[k, d], (twin, zme)
        )

    def weight_part(i):
        part = lax.dot_general(
            tokg_ref[...], grads[i], (((0,), (0,)), ((), ())), preferred_element_type=F32
        )
        wacc[i] = part
        wsend[i] = part.astype(BF16)

    greet(S, Z, sme, zme)
    if H == 2:
        d_copy().start()
    for d in range(1, Z):
        k_copy(d).start()
    half = first_half((R, LANES))
    own = do_ref[hme]
    if H == 2:
        d_copy().wait_recv()
        other = dbuf[...]
        even = jnp.where(hme == 0, own, other)
        odd = jnp.where(hme == 0, other, own)
        grads[0] = jnp.where(half, even, odd)
        osend[...] = turn(jnp.where(half, odd, even))
    else:
        grads[0] = jnp.where(half, own, jnp.zeros_like(own))
        osend[...] = own
    for d in range(1, S):
        o_copy(d, sme).start()
    att[sme] = osend[rows(sme), :]
    weight_part(0)
    for d in range(1, Z):
        w_copy(d, 0).start()
    for d in range(1, Z):
        k_copy(d).wait_recv()
    for h in range(H):
        total = dkv_ref[zme].astype(F32) if h == 0 else None
        for d in range(1, Z):
            if d % H == h:
                term = kbuf[d - 1].astype(F32)
                total = term if total is None else total + term
        grads[1 + lax.rem(hme + h, H)] = total.astype(BF16)
    for h in range(H):
        weight_part(1 + h)
        for d in range(1, Z):
            w_copy(d, 1 + h).start()

    def weight_sum(i):
        for d in range(1, Z):
            w_copy(d, i).wait_recv()
        total = wacc[i, wrows(zme), :]
        for d in range(1, Z):
            total += wbuf[d - 1, i].astype(F32)
        return total

    def share(k):
        for d in range(1, C):
            g_copy(k, d, sme).start()
        f_copy(k, 0, core).start()

    def forward(k):
        for d in range(1, C):
            g_copy(k, d, back(d) * 2 + core).wait_recv()
            f_copy(k, d, core).start()

    wo[sme, 0] = weight_sum(0).astype(BF16)
    share(0)

    def token_part(block):
        total = None
        for i in range(1 + H):
            term = lax.dot_general(
                grads[i, rows(block), :], wg_ref[i], (((1,), (1,)), ((), ())),
                preferred_element_type=F32,
            )
            total = term if total is None else total + term
        return total

    def twin_part(j, carry):
        d = lax.rem(j + 1, C)
        csend[d] = token_part(there(d) * 2 + 1 - core).astype(BF16)
        c_copy(d).start()
        return carry

    lax.fori_loop(0, C, twin_part, 0)

    def own_part(d, carry):
        total = token_part(there(d) * 2 + core)
        c_copy(d).wait_recv()
        tsend[d - 1] = (total + cbuf[d].astype(F32)).astype(BF16)
        t_copy(d).start()
        return carry

    lax.fori_loop(1, C, own_part, 0)
    part[...] = token_part(sme)
    c_copy(0).wait_recv()
    part[...] += cbuf[0].astype(F32)
    forward(0)
    sums = [weight_sum(1 + h) for h in range(H)]
    if H == 2:
        cut = first_half((W, LANES))
        value = pltpu.roll(jnp.where(cut, sums[1], sums[0]), HEAD, 1)
        sums = [jnp.where(cut, sums[0], sums[1]), value]
    for h in range(H):
        wo[sme, 1 + h] = sums[h].astype(BF16)
    share(1)
    for d in range(1, C):
        t_copy(d).wait_recv()
        part[...] += tbuf[d - 1].astype(F32)
    tg_ref[...] = part[...].astype(BF16)
    for d in range(1, S):
        o_copy(d, sfrom(d)).wait_recv()
    for p in range(S):
        block = att[p]
        att_ref[:, p * hc : (p + 1) * hc] = block if H == 2 else block[:, HEAD:]
    forward(1)
    for k in range(2):
        for d in range(C):
            f_copy(k, d, 1 - core).wait_recv()
        for p in range(S):
            for i in range(3) if H == 2 else ():
                if (k == 0) == (i == 0):
                    lo = (i * S + p) * hc
                    wout_ref[:, lo : lo + hc] = wo[p, i].astype(F32)
    if H == 1:
        for p in range(S):
            both = wo[p, 1].astype(F32)
            three = [wo[p, 0].astype(F32)[:, :HEAD], both[:, :HEAD], both[:, HEAD:]]
            for i in range(3):
                lo = (i * S + p) * hc
                wout_ref[:, lo : lo + hc] = three[i]
    if H == 2:
        d_copy().wait_send()
    for d in range(1, Z):
        k_copy(d).wait_send()
        for i in range(1 + H):
            w_copy(d, i).wait_send()
    for d in range(1, S):
        o_copy(d, sme).wait_send()
    for d in range(C):
        c_copy(d).wait_send()
        for k in range(2):
            f_copy(k, d, core).wait_send()
        if d:
            t_copy(d).wait_send()
            for k in range(2):
                g_copy(k, d, sme).wait_send()


def dma(*shape):
    return pltpu.SemaphoreType.DMA(shape)


def on_device(tokens, projection, pattern, upstream):
    S = lax.axis_size("seq")
    Z = lax.axis_size("zero")
    T, D = tokens.shape
    hc = HEADS // S * HEAD
    W = projection.shape[0]
    R = S * T
    per_shard = T // BLOCK
    H = hc // HEAD
    total = Z * S * per_shard
    shape = jax.ShapeDtypeStruct
    own, up = projection, upstream
    if H == 1:
        own = lax.dynamic_index_in_dim(
            projection.reshape(W, 3, S, hc), lax.axis_index("seq"), axis=2, keepdims=False
        )
        own = own.transpose(1, 0, 2)
        up = upstream.reshape(T, S, hc).transpose(1, 0, 2)
        own = jnp.stack(
            [
                jnp.concatenate([own[0], jnp.zeros_like(own[0])], axis=1),
                jnp.concatenate([own[1], own[2]], axis=1),
            ]
        )
        up = jnp.concatenate([jnp.zeros_like(up), up], axis=2)
    tokg, wg, kv, qu = pl.pallas_call(
        functools.partial(gather_kernel, S, Z, H),
        out_shape=(
            shape((R, D), BF16), shape((1 + H, D, LANES), BF16),
            shape((Z, R, LANES), BF16), shape((H, R, LANES), BF16),
        ),
        in_specs=[VMEM, pl.BlockSpec(memory_space=pl.ANY) if H == 2 else VMEM, VMEM],
        out_specs=(VMEM,) * 4,
        scratch_shapes=[
            pltpu.VMEM((3, W, LANES), BF16),
            dma(3),
            pltpu.VMEM((1 + H, W, LANES), BF16),
            pltpu.VMEM((H, R, LANES), BF16),
            pltpu.VMEM((H, R, LANES), BF16),
            pltpu.VMEM((R, LANES), BF16),
            dma(S), dma(S), dma(Z), dma(Z), dma(S), dma(S), dma(Z, S), dma(Z, S), dma(S), dma(S),
        ],
        compiler_params=pltpu.CompilerParams(
            collective_id=0, has_side_effects=True, vmem_limit_bytes=LIMIT
        ),
        name="gather",
    )(tokens, own, up)
    do, dkv = pl.pallas_call(
        functools.partial(attend_kernel, S, Z, H, per_shard),
        out_shape=(
            shape((H * S * per_shard, BLOCK, LANES), BF16), shape((total, BLOCK, LANES), BF16),
        ),
        in_specs=[SMEM] + [VMEM] * 2,
        out_specs=(VMEM,) * 2,
        scratch_shapes=[pltpu.VMEM((total, BLOCK, LANES), F32)],
        compiler_params=pltpu.CompilerParams(vmem_limit_bytes=LIMIT),
        name="attend",
    )(
        pattern,
        qu.reshape(H * S * per_shard, BLOCK, LANES),
        kv.reshape(total, BLOCK, LANES),
    )
    att, tg, wo = pl.pallas_call(
        functools.partial(reduce_kernel, S, Z, H),
        out_shape=(
            shape((T, S * hc), BF16), shape((T, D), BF16), shape((W, 3 * S * hc), F32),
        ),
        in_specs=[VMEM] * 4,
        out_specs=(VMEM,) * 3,
        scratch_shapes=[
            pltpu.VMEM((R, LANES), BF16),
            pltpu.VMEM((R, LANES), BF16),
            pltpu.VMEM((Z - 1, R, LANES), BF16),
            pltpu.VMEM((1 + H, R, LANES), BF16),
            pltpu.VMEM((1 + H, D, LANES), F32),
            pltpu.VMEM((1 + H, D, LANES), BF16),
            pltpu.VMEM((Z - 1, 1 + H, W, LANES), BF16),
            pltpu.VMEM((S, 1 + H, W, LANES), BF16),
            pltpu.VMEM((S, T, LANES), BF16),
            pltpu.VMEM((T, D), F32),
            pltpu.VMEM((S // 2, T, D), BF16),
            pltpu.VMEM((S // 2, T, D), BF16),
            pltpu.VMEM((S // 2 - 1, T, D), BF16),
            pltpu.VMEM((S // 2 - 1, T, D), BF16),
            pltpu.SemaphoreType.DMA, pltpu.SemaphoreType.DMA,
            dma(S), dma(S), dma(Z), dma(Z), dma(Z, 1 + H), dma(Z, 1 + H),
            dma(S // 2), dma(S // 2), dma(S // 2), dma(S // 2),
            dma(2, S // 2), dma(2, S // 2), dma(2, S // 2), dma(2, S // 2),
        ],
        compiler_params=pltpu.CompilerParams(
            collective_id=1, has_side_effects=True, vmem_limit_bytes=LIMIT
        ),
        name="reduce",
    )(do.reshape(H, R, LANES), dkv.reshape(Z, R, LANES), tokg, wg)
    return (att, tg, wo)


def solution(mesh):
    return jax.shard_map(
        on_device,
        mesh=mesh,
        in_specs=(P(("seq", "zero"), None), P("zero", None), P(), P(("seq", "zero"), None)),
        out_specs=(P(("seq", "zero"), None), P(("seq", "zero"), None), P("zero", None)),
        check_vma=False,
    )
```

```python
import functools

import jax
import jax.numpy as jnp
from jax import lax
from jax.experimental import pallas as pl
from jax.experimental.pallas import tpu as pltpu
from jax.sharding import PartitionSpec as P

HEADS = 16
HEAD = 64
BLOCK = 128
NBK = 8
LANES = 128
MESH = pl.DeviceIdType.MESH
F32 = jnp.float32
BF16 = jnp.bfloat16
VMEM = pl.BlockSpec(memory_space=pltpu.VMEM)
SMEM = pl.BlockSpec(memory_space=pltpu.SMEM)
LIMIT = 56 * 1024 * 1024


def remote(src, dst, send, recv, where):
    return pltpu.make_async_remote_copy(
        src_ref=src, dst_ref=dst, send_sem=send, recv_sem=recv, device_id=where, device_id_type=MESH
    )


def greet(S, Z, sme, zme):
    barrier = pltpu.get_barrier_semaphore()
    for d in range(1, S):
        pl.semaphore_signal(
            barrier, inc=1, device_id=(lax.rem(sme + d, S), zme), device_id_type=MESH
        )
    for d in range(1, Z):
        pl.semaphore_signal(
            barrier, inc=1, device_id=(sme, lax.rem(zme + d, Z)), device_id_type=MESH
        )
    pl.semaphore_wait(barrier, S + Z - 2)


def turn(x):
    return pltpu.roll(x.astype(F32), HEAD, 1).astype(BF16)


def first_half(shape):
    return lax.broadcasted_iota(jnp.int32, shape, 1) < HEAD


def gather_kernel(
    S, Z, H, tok_ref, w_ref, up_ref, tokg_ref, wg_ref, kv_ref, qu_ref,
    wraw, wsem, wown, kvown, quown, ubuf, ts, tr, ws, wr, us, ur, ks, kr, qs, qr,
):
    sme, zme = lax.axis_index("seq"), lax.axis_index("zero")
    hme = lax.rem(zme, H)
    mate = zme + 1 - 2 * hme
    T = tok_ref.shape[0]
    W = wown.shape[1]

    def rows(i):
        return pl.ds(pl.multiple_of(i * T, T), T)

    def wrows(i):
        return pl.ds(pl.multiple_of(i * W, W), W)

    def up_part(peer):
        if H == 1:
            return up_ref.at[peer]
        return up_ref.at[:, pl.ds(pl.multiple_of(peer * LANES, LANES), LANES)]

    def raw_copy(i):
        at = pl.ds(pl.multiple_of((i * S + sme) * LANES, LANES), LANES)
        return pltpu.make_async_copy(w_ref.at[:, at], wraw.at[i], wsem.at[i])

    def w_copy(d, owner, peer):
        return remote(wown, wg_ref.at[:, wrows(owner)], ws.at[d], wr.at[d], (sme, peer))

    def t_copy(d, owner, peer):
        return remote(tok_ref, tokg_ref.at[rows(owner)], ts.at[d], tr.at[d], (peer, zme))

    def u_copy(d, owner, peer):
        return remote(up_part(peer), ubuf.at[rows(owner)], us.at[d], ur.at[d], (peer, zme))

    def k_copy(zd, d, owner, peer, block):
        src = kvown.at[lax.rem(peer, H), rows(block)]
        return remote(src, kv_ref.at[owner, rows(block)], ks.at[zd, d], kr.at[zd, d], (sme, peer))

    def q_copy(d, group, block):
        src = quown.at[1 - hme, rows(block)]
        return remote(src, qu_ref.at[group, rows(block)], qs.at[d], qr.at[d], (sme, mate))

    if H == 2:
        for i in range(3):
            raw_copy(i).start()
        for i in range(3):
            raw_copy(i).wait()
        half = first_half((W, LANES))
        turned = turn(wraw[2])
        wown[0] = wraw[0]
        wown[1] = jnp.where(half, wraw[1], turned)
        wown[2] = jnp.where(half, turned, wraw[1])
    else:
        wown[...] = w_ref[...]
    greet(S, Z, sme, zme)
    for d in range(1, Z):
        w_copy(d, zme, lax.rem(zme + d, Z)).start()
    for d in range(1, S):
        peer = lax.rem(sme + d, S)
        t_copy(d, sme, peer).start()
        u_copy(d, sme, peer).start()
    wg_ref[:, wrows(zme), :] = wown[...]
    tokg_ref[rows(sme), :] = tok_ref[...]
    if H == 1:
        ubuf[rows(sme), :] = up_ref[sme]
    else:
        ubuf[rows(sme), :] = up_ref[:, pl.ds(pl.multiple_of(sme * LANES, LANES), LANES)]
    for d in range(1, Z):
        w_copy(d, lax.rem(zme + Z - d, Z), lax.rem(zme + d, Z)).wait_recv()

    def project(d):
        block = lax.rem(sme + S - d, S)
        here = tokg_ref[rows(block), :]
        for h in range(H):
            kvown[h, rows(block), :] = jnp.dot(
                here, wg_ref[h + 1], preferred_element_type=F32
            ).astype(BF16)
        for zd in range(1, Z):
            k_copy(zd, d, zme, lax.rem(zme + zd, Z), block).start()
        kv_ref[zme, rows(block), :] = kvown[hme, rows(block), :]
        queries = jnp.dot(here, wg_ref[0], preferred_element_type=F32).astype(BF16)
        half = first_half((T, LANES))
        if H == 2:
            ups = turn(ubuf[rows(block), :])
            quown[0, rows(block), :] = jnp.where(half, queries, ups)
            quown[1, rows(block), :] = jnp.where(half, ups, queries)
            q_copy(d, hme, block).start()
        else:
            quown[0, rows(block), :] = jnp.where(half, queries, ubuf[rows(block), :])
        qu_ref[hme, rows(block), :] = quown[hme, rows(block), :]

    project(0)

    def step(d, carry):
        owner, peer = lax.rem(sme + S - d, S), lax.rem(sme + d, S)
        t_copy(d, owner, peer).wait_recv()
        u_copy(d, owner, peer).wait_recv()
        project(d)
        return carry

    lax.fori_loop(1, S, step, 0)

    def finish(d, carry):
        block = lax.rem(sme + S - d, S)
        for zd in range(1, Z):
            peer = lax.rem(zme + zd, Z)
            k_copy(zd, d, lax.rem(zme + Z - zd, Z), peer, block).wait_recv()
            k_copy(zd, d, zme, peer, block).wait_send()
        if H == 2:
            q_copy(d, 1 - hme, block).wait_recv()
            q_copy(d, hme, block).wait_send()
        return carry

    for d in range(1, S):
        peer = lax.rem(sme + d, S)
        u_copy(d, sme, peer).wait_send()
        t_copy(d, sme, peer).wait_send()
    for d in range(1, Z):
        w_copy(d, zme, lax.rem(zme + d, Z)).wait_send()
    lax.fori_loop(0, S, finish, 0)


def attend_kernel(S, Z, H, per_shard, pat_ref, qu_ref, kv_ref, do_ref, dkv_ref, acc):
    zme = lax.axis_index("zero")
    hme = zme % H
    local = S * per_shard
    total = Z * local
    scale = HEAD ** (-0.5)

    def clear(i, carry):
        acc[i] = jnp.zeros((BLOCK, LANES), F32)
        return carry

    lax.fori_loop(0, total, clear, 0)
    is_q = lax.broadcasted_iota(jnp.int32, (BLOCK, LANES), 1) // HEAD == hme
    is_dq = lax.broadcasted_iota(jnp.int32, (LANES, BLOCK), 0) // HEAD == hme

    def nt(x, y):
        return lax.dot_general(x, y, (((1,), (1,)), ((), ())), preferred_element_type=F32)

    def begin(i):
        r = i % local
        row = (r // per_shard * Z + zme - hme + i // local) * per_shard + r % per_shard
        slots = []
        for j in range(NBK):
            b = pat_ref[row, j]
            shard = b // per_shard
            slots.append(shard % Z * local + shard // Z * per_shard + b % per_shard)
        qu = qu_ref[i]
        none = jnp.zeros_like(qu)
        both = jnp.concatenate([jnp.where(is_q, qu, none), jnp.where(is_q, none, qu)], axis=0)
        keys = jnp.concatenate([kv_ref[s] for s in slots], axis=0)
        return slots, both, keys, nt(keys, both)

    def soften(mixed):
        scores = mixed[:, :BLOCK] * scale
        grad = mixed[:, BLOCK:]
        top = jnp.max(scores, axis=0, keepdims=True)
        exponent = jnp.exp(scores - top)
        inverse = 1.0 / jnp.sum(exponent, axis=0, keepdims=True)
        delta = jnp.sum(exponent * grad, axis=0, keepdims=True) * inverse
        low = (exponent * inverse).astype(BF16)
        sg = (exponent * (inverse * scale) * (grad - delta)).astype(BF16)
        return jnp.concatenate([sg, low], axis=1)

    def end(i, slots, both, keys, pair):
        outs = lax.dot_general(keys, pair, (((0,), (0,)), ((), ())), preferred_element_type=F32)
        do_ref[i] = jnp.where(is_dq, outs[:, :BLOCK], outs[:, BLOCK:]).T.astype(BF16)
        terms = jnp.dot(pair, both, preferred_element_type=F32)
        for j in range(NBK):
            acc[slots[j]] += terms[j * BLOCK : (j + 1) * BLOCK]

    def step(t, carry):
        one, two = 2 * t, 2 * t + 1
        slots_one, both_one, keys_one, mixed_one = begin(one)
        slots_two, both_two, keys_two, mixed_two = begin(two)
        pair_one = soften(mixed_one)
        pair_two = soften(mixed_two)
        end(one, slots_one, both_one, keys_one, pair_one)
        end(two, slots_two, both_two, keys_two, pair_two)
        return carry

    lax.fori_loop(0, H * local // 2, step, 0)

    def store(i, carry):
        dkv_ref[i] = acc[i].astype(BF16)
        return carry

    lax.fori_loop(0, total, store, 0)


def reduce_kernel(
    S, Z, H, do_ref, dkv_ref, tokg_ref, wg_ref, att_ref, tg_ref, wout_ref,
    dbuf, osend, kbuf, grads, wacc, wsend, wbuf, wo, att, part, csend, cbuf, tsend, tbuf,
    ds, dr, os, orr, ks, kr, ws, wr, cs, cr, ts, tr, gs, gr, fs, fr,
):
    sme, zme = lax.axis_index("seq"), lax.axis_index("zero")
    hme = lax.rem(zme, H)
    mate = zme + 1 - 2 * hme
    C = S // 2
    core = lax.rem(sme, 2)
    chip = sme // 2
    twin = sme + 1 - 2 * core
    T = tg_ref.shape[0]
    W = wo.shape[2]
    R = S * T
    hc = H * HEAD

    def rows(i):
        return pl.ds(pl.multiple_of(i * T, T), T)

    def wrows(i):
        return pl.ds(pl.multiple_of(i * W, W), W)

    def speer(d):
        return lax.rem(sme + d, S)

    def sfrom(d):
        return lax.rem(sme + S - d, S)

    def zpeer(d):
        return lax.rem(zme + d, Z)

    def d_copy():
        return remote(do_ref.at[1 - hme], dbuf, ds, dr, (sme, mate))

    def k_copy(d):
        return remote(dkv_ref.at[zpeer(d)], kbuf.at[d - 1], ks.at[d], kr.at[d], (sme, zpeer(d)))

    def there(d):
        return lax.rem(chip + d, C)

    def back(d):
        return lax.rem(chip + C - d, C)

    def o_copy(d, owner):
        return remote(
            osend.at[rows(speer(d))], att.at[owner], os.at[d], orr.at[d], (speer(d), zme)
        )

    def w_copy(d, i):
        return remote(
            wsend.at[i, wrows(zpeer(d))], wbuf.at[d - 1, i], ws.at[d, i], wr.at[d, i],
            (sme, zpeer(d)),
        )

    def c_copy(d):
        return remote(csend.at[d], cbuf.at[d], cs.at[d], cr.at[d], (twin, zme))

    def t_copy(d):
        return remote(
            tsend.at[d - 1], tbuf.at[d - 1], ts.at[d], tr.at[d], (there(d) * 2 + core, zme)
        )

    def span(k):
        return pl.ds(0, 1) if k == 0 else pl.ds(1, wo.shape[1] - 1)

    def g_copy(k, d, owner):
        block = wo.at[sme, span(k)]
        return remote(
            block, wo.at[owner, span(k)], gs.at[k, d], gr.at[k, d], (there(d) * 2 + core, zme)
        )

    def f_copy(k, d, side):
        block = wo.at[back(d) * 2 + core, span(k)]
        return remote(
            block, wo.at[back(d) * 2 + side, span(k)], fs.at[k, d], fr.at[k, d], (twin, zme)
        )

    def weight_part(i):
        part = lax.dot_general(
            tokg_ref[...], grads[i], (((0,), (0,)), ((), ())), preferred_element_type=F32
        )
        wacc[i] = part
        wsend[i] = part.astype(BF16)

    greet(S, Z, sme, zme)
    if H == 2:
        d_copy().start()
    for d in range(1, Z):
        k_copy(d).start()
    half = first_half((R, LANES))
    own = do_ref[hme]
    if H == 2:
        d_copy().wait_recv()
        other = dbuf[...]
        even = jnp.where(hme == 0, own, other)
        odd = jnp.where(hme == 0, other, own)
        grads[0] = jnp.where(half, even, odd)
        osend[...] = turn(jnp.where(half, odd, even))
    else:
        grads[0] = jnp.where(half, own, jnp.zeros_like(own))
        osend[...] = own
    for d in range(1, S):
        o_copy(d, sme).start()
    att[sme] = osend[rows(sme), :]
    weight_part(0)
    for d in range(1, Z):
        w_copy(d, 0).start()
    for d in range(1, Z):
        k_copy(d).wait_recv()
    for h in range(H):
        total = dkv_ref[zme].astype(F32) if h == 0 else None
        for d in range(1, Z):
            if d % H == h:
                term = kbuf[d - 1].astype(F32)
                total = term if total is None else total + term
        grads[1 + lax.rem(hme + h, H)] = total.astype(BF16)
    for h in range(H):
        weight_part(1 + h)
        for d in range(1, Z):
            w_copy(d, 1 + h).start()

    def weight_sum(i):
        for d in range(1, Z):
            w_copy(d, i).wait_recv()
        total = wacc[i, wrows(zme), :]
        for d in range(1, Z):
            total += wbuf[d - 1, i].astype(F32)
        return total

    def share(k):
        for d in range(1, C):
            g_copy(k, d, sme).start()
        f_copy(k, 0, core).start()

    def forward(k):
        for d in range(1, C):
            g_copy(k, d, back(d) * 2 + core).wait_recv()
            f_copy(k, d, core).start()

    wo[sme, 0] = weight_sum(0).astype(BF16)
    share(0)

    def token_part(block):
        total = None
        for i in range(1 + H):
            term = lax.dot_general(
                grads[i, rows(block), :], wg_ref[i], (((1,), (1,)), ((), ())),
                preferred_element_type=F32,
            )
            total = term if total is None else total + term
        return total

    def twin_part(j, carry):
        d = lax.rem(j + 1, C)
        csend[d] = token_part(there(d) * 2 + 1 - core).astype(BF16)
        c_copy(d).start()
        return carry

    lax.fori_loop(0, C, twin_part, 0)

    def own_part(d, carry):
        total = token_part(there(d) * 2 + core)
        c_copy(d).wait_recv()
        tsend[d - 1] = (total + cbuf[d].astype(F32)).astype(BF16)
        t_copy(d).start()
        return carry

    lax.fori_loop(1, C, own_part, 0)
    part[...] = token_part(sme)
    c_copy(0).wait_recv()
    part[...] += cbuf[0].astype(F32)
    forward(0)
    sums = [weight_sum(1 + h) for h in range(H)]
    if H == 2:
        cut = first_half((W, LANES))
        value = pltpu.roll(jnp.where(cut, sums[1], sums[0]), HEAD, 1)
        sums = [jnp.where(cut, sums[0], sums[1]), value]
    for h in range(H):
        wo[sme, 1 + h] = sums[h].astype(BF16)
    share(1)
    for d in range(1, C):
        t_copy(d).wait_recv()
        part[...] += tbuf[d - 1].astype(F32)
    tg_ref[...] = part[...].astype(BF16)
    for d in range(1, S):
        o_copy(d, sfrom(d)).wait_recv()
    for p in range(S):
        block = att[p]
        att_ref[:, p * hc : (p + 1) * hc] = block if H == 2 else block[:, HEAD:]
    forward(1)
    for k in range(2):
        for d in range(C):
            f_copy(k, d, 1 - core).wait_recv()
        for p in range(S):
            for i in range(3) if H == 2 else ():
                if (k == 0) == (i == 0):
                    lo = (i * S + p) * hc
                    wout_ref[:, lo : lo + hc] = wo[p, i]
    if H == 1:
        for p in range(S):
            both = wo[p, 1].astype(F32)
            three = [wo[p, 0].astype(F32)[:, :HEAD], both[:, :HEAD], both[:, HEAD:]]
            for i in range(3):
                lo = (i * S + p) * hc
                wout_ref[:, lo : lo + hc] = three[i].astype(BF16)
    if H == 2:
        d_copy().wait_send()
    for d in range(1, Z):
        k_copy(d).wait_send()
        for i in range(1 + H):
            w_copy(d, i).wait_send()
    for d in range(1, S):
        o_copy(d, sme).wait_send()
    for d in range(C):
        c_copy(d).wait_send()
        for k in range(2):
            f_copy(k, d, core).wait_send()
        if d:
            t_copy(d).wait_send()
            for k in range(2):
                g_copy(k, d, sme).wait_send()


def dma(*shape):
    return pltpu.SemaphoreType.DMA(shape)


def on_device(tokens, projection, pattern, upstream):
    S = lax.axis_size("seq")
    Z = lax.axis_size("zero")
    T, D = tokens.shape
    hc = HEADS // S * HEAD
    W = projection.shape[0]
    R = S * T
    per_shard = T // BLOCK
    H = hc // HEAD
    total = Z * S * per_shard
    shape = jax.ShapeDtypeStruct
    own, up = projection, upstream
    if H == 1:
        own = lax.dynamic_index_in_dim(
            projection.reshape(W, 3, S, hc), lax.axis_index("seq"), axis=2, keepdims=False
        )
        own = own.transpose(1, 0, 2)
        up = upstream.reshape(T, S, hc).transpose(1, 0, 2)
        own = jnp.stack(
            [
                jnp.concatenate([own[0], jnp.zeros_like(own[0])], axis=1),
                jnp.concatenate([own[1], own[2]], axis=1),
            ]
        )
        up = jnp.concatenate([jnp.zeros_like(up), up], axis=2)
    tokg, wg, kv, qu = pl.pallas_call(
        functools.partial(gather_kernel, S, Z, H),
        out_shape=(
            shape((R, D), BF16), shape((1 + H, D, LANES), BF16),
            shape((Z, R, LANES), BF16), shape((H, R, LANES), BF16),
        ),
        in_specs=[VMEM, pl.BlockSpec(memory_space=pl.ANY) if H == 2 else VMEM, VMEM],
        out_specs=(VMEM,) * 4,
        scratch_shapes=[
            pltpu.VMEM((3, W, LANES), BF16),
            dma(3),
            pltpu.VMEM((1 + H, W, LANES), BF16),
            pltpu.VMEM((H, R, LANES), BF16),
            pltpu.VMEM((H, R, LANES), BF16),
            pltpu.VMEM((R, LANES), BF16),
            dma(S), dma(S), dma(Z), dma(Z), dma(S), dma(S), dma(Z, S), dma(Z, S), dma(S), dma(S),
        ],
        compiler_params=pltpu.CompilerParams(
            collective_id=0, has_side_effects=True, vmem_limit_bytes=LIMIT
        ),
        name="gather",
    )(tokens, own, up)
    do, dkv = pl.pallas_call(
        functools.partial(attend_kernel, S, Z, H, per_shard),
        out_shape=(
            shape((H * S * per_shard, BLOCK, LANES), BF16), shape((total, BLOCK, LANES), BF16),
        ),
        in_specs=[SMEM] + [VMEM] * 2,
        out_specs=(VMEM,) * 2,
        scratch_shapes=[pltpu.VMEM((total, BLOCK, LANES), F32)],
        compiler_params=pltpu.CompilerParams(vmem_limit_bytes=LIMIT),
        name="attend",
    )(
        pattern,
        qu.reshape(H * S * per_shard, BLOCK, LANES),
        kv.reshape(total, BLOCK, LANES),
    )
    att, tg, wo = pl.pallas_call(
        functools.partial(reduce_kernel, S, Z, H),
        out_shape=(
            shape((T, S * hc), BF16), shape((T, D), BF16), shape((W, 3 * S * hc), BF16),
        ),
        in_specs=[VMEM] * 4,
        out_specs=(VMEM,) * 3,
        scratch_shapes=[
            pltpu.VMEM((R, LANES), BF16),
            pltpu.VMEM((R, LANES), BF16),
            pltpu.VMEM((Z - 1, R, LANES), BF16),
            pltpu.VMEM((1 + H, R, LANES), BF16),
            pltpu.VMEM((1 + H, D, LANES), F32),
            pltpu.VMEM((1 + H, D, LANES), BF16),
            pltpu.VMEM((Z - 1, 1 + H, W, LANES), BF16),
            pltpu.VMEM((S, 1 + H, W, LANES), BF16),
            pltpu.VMEM((S, T, LANES), BF16),
            pltpu.VMEM((T, D), F32),
            pltpu.VMEM((S // 2, T, D), BF16),
            pltpu.VMEM((S // 2, T, D), BF16),
            pltpu.VMEM((S // 2 - 1, T, D), BF16),
            pltpu.VMEM((S // 2 - 1, T, D), BF16),
            pltpu.SemaphoreType.DMA, pltpu.SemaphoreType.DMA,
            dma(S), dma(S), dma(Z), dma(Z), dma(Z, 1 + H), dma(Z, 1 + H),
            dma(S // 2), dma(S // 2), dma(S // 2), dma(S // 2),
            dma(2, S // 2), dma(2, S // 2), dma(2, S // 2), dma(2, S // 2),
        ],
        compiler_params=pltpu.CompilerParams(
            collective_id=1, has_side_effects=True, vmem_limit_bytes=LIMIT
        ),
        name="reduce",
    )(do.reshape(H, R, LANES), dkv.reshape(Z, R, LANES), tokg, wg)
    return (att, tg, wo.astype(F32))


def solution(mesh):
    return jax.shard_map(
        on_device,
        mesh=mesh,
        in_specs=(P(("seq", "zero"), None), P("zero", None), P(), P(("seq", "zero"), None)),
        out_specs=(P(("seq", "zero"), None), P(("seq", "zero"), None), P("zero", None)),
        check_vma=False,
    )
```

```python
import functools

import jax
import jax.numpy as jnp
from jax import lax
from jax.experimental import pallas as pl
from jax.experimental.pallas import tpu as pltpu
from jax.sharding import PartitionSpec as P

HEADS = 16
HEAD = 64
BLOCK = 128
NBK = 8
LANES = 128
MESH = pl.DeviceIdType.MESH
F32 = jnp.float32
BF16 = jnp.bfloat16
VMEM = pl.BlockSpec(memory_space=pltpu.VMEM)
SMEM = pl.BlockSpec(memory_space=pltpu.SMEM)
LIMIT = 56 * 1024 * 1024


def remote(src, dst, send, recv, where):
    return pltpu.make_async_remote_copy(
        src_ref=src, dst_ref=dst, send_sem=send, recv_sem=recv, device_id=where, device_id_type=MESH
    )


def greet(S, Z, sme, zme):
    barrier = pltpu.get_barrier_semaphore()
    for d in range(1, S):
        pl.semaphore_signal(
            barrier, inc=1, device_id=(lax.rem(sme + d, S), zme), device_id_type=MESH
        )
    for d in range(1, Z):
        pl.semaphore_signal(
            barrier, inc=1, device_id=(sme, lax.rem(zme + d, Z)), device_id_type=MESH
        )
    pl.semaphore_wait(barrier, S + Z - 2)


def turn(x):
    return pltpu.roll(x.astype(F32), HEAD, 1).astype(BF16)


def first_half(shape):
    return lax.broadcasted_iota(jnp.int32, shape, 1) < HEAD


def gather_kernel(
    S, Z, H, tok_ref, w_ref, up_ref, tokg_ref, wg_ref, kv_ref, qu_ref,
    wraw, wsem, wown, kvown, quown, ubuf, ts, tr, ws, wr, us, ur, ks, kr, qs, qr,
):
    sme, zme = lax.axis_index("seq"), lax.axis_index("zero")
    hme = lax.rem(zme, H)
    mate = zme + 1 - 2 * hme
    T = tok_ref.shape[0]
    W = wown.shape[1]

    def rows(i):
        return pl.ds(pl.multiple_of(i * T, T), T)

    def wrows(i):
        return pl.ds(pl.multiple_of(i * W, W), W)

    def up_part(peer):
        if H == 1:
            return up_ref.at[peer]
        return up_ref.at[:, pl.ds(pl.multiple_of(peer * LANES, LANES), LANES)]

    def raw_copy(i):
        at = pl.ds(pl.multiple_of((i * S + sme) * LANES, LANES), LANES)
        return pltpu.make_async_copy(w_ref.at[:, at], wraw.at[i], wsem.at[i])

    def w_copy(d, owner, peer):
        return remote(wown, wg_ref.at[:, wrows(owner)], ws.at[d], wr.at[d], (sme, peer))

    C = S // 2
    core = lax.rem(sme, 2)
    chip = sme // 2
    twin = sme + 1 - 2 * core

    def owner_at(c, side):
        return lax.rem(chip + C - c, C) * 2 + side

    def t_copy(c, owner):
        peer = lax.rem(chip + c, C) * 2 + core
        return remote(tok_ref, tokg_ref.at[rows(owner)], ts.at[c], tr.at[c], (peer, zme))

    def f_copy(c, side):
        src = tokg_ref.at[rows(owner_at(c, core))]
        dst = tokg_ref.at[rows(owner_at(c, side))]
        return remote(src, dst, ts.at[C + c], tr.at[C + c], (twin, zme))

    def u_copy(d, owner, peer):
        return remote(up_part(peer), ubuf.at[rows(owner)], us.at[d], ur.at[d], (peer, zme))

    def k_copy(zd, d, owner, peer, block):
        src = kvown.at[lax.rem(peer, H), rows(block)]
        return remote(src, kv_ref.at[owner, rows(block)], ks.at[zd, d], kr.at[zd, d], (sme, peer))

    def q_copy(d, group, block):
        src = quown.at[1 - hme, rows(block)]
        return remote(src, qu_ref.at[group, rows(block)], qs.at[d], qr.at[d], (sme, mate))

    if H == 2:
        for i in range(3):
            raw_copy(i).start()
        for i in range(3):
            raw_copy(i).wait()
        half = first_half((W, LANES))
        turned = turn(wraw[2])
        wown[0] = wraw[0]
        wown[1] = jnp.where(half, wraw[1], turned)
        wown[2] = jnp.where(half, turned, wraw[1])
    else:
        wown[...] = w_ref[...]
    greet(S, Z, sme, zme)
    for d in range(1, Z):
        w_copy(d, zme, lax.rem(zme + d, Z)).start()
    tokg_ref[rows(sme), :] = tok_ref[...]
    for c in range(1, C):
        t_copy(c, sme).start()
    f_copy(0, core).start()
    for d in range(1, S):
        u_copy(d, sme, lax.rem(sme + d, S)).start()
    wg_ref[:, wrows(zme), :] = wown[...]
    if H == 1:
        ubuf[rows(sme), :] = up_ref[sme]
    else:
        ubuf[rows(sme), :] = up_ref[:, pl.ds(pl.multiple_of(sme * LANES, LANES), LANES)]
    for d in range(1, Z):
        w_copy(d, lax.rem(zme + Z - d, Z), lax.rem(zme + d, Z)).wait_recv()

    def project(block):
        d = lax.rem(sme + S - block, S)
        here = tokg_ref[rows(block), :]
        for h in range(H):
            kvown[h, rows(block), :] = jnp.dot(
                here, wg_ref[h + 1], preferred_element_type=F32
            ).astype(BF16)
        for zd in range(1, Z):
            k_copy(zd, d, zme, lax.rem(zme + zd, Z), block).start()
        kv_ref[zme, rows(block), :] = kvown[hme, rows(block), :]
        queries = jnp.dot(here, wg_ref[0], preferred_element_type=F32).astype(BF16)
        half = first_half((T, LANES))
        if H == 2:
            ups = turn(ubuf[rows(block), :])
            quown[0, rows(block), :] = jnp.where(half, queries, ups)
            quown[1, rows(block), :] = jnp.where(half, ups, queries)
            q_copy(d, hme, block).start()
        else:
            quown[0, rows(block), :] = jnp.where(half, queries, ubuf[rows(block), :])
        qu_ref[hme, rows(block), :] = quown[hme, rows(block), :]

    def upstream_of(block):
        d = lax.rem(sme + S - block, S)
        u_copy(d, block, lax.rem(sme + d, S)).wait_recv()

    project(sme)
    f_copy(0, 1 - core).wait_recv()
    upstream_of(twin)
    project(twin)

    def step(c, carry):
        same, across = owner_at(c, core), owner_at(c, 1 - core)
        t_copy(c, same).wait_recv()
        f_copy(c, core).start()
        upstream_of(same)
        project(same)
        f_copy(c, 1 - core).wait_recv()
        upstream_of(across)
        project(across)
        return carry

    lax.fori_loop(1, C, step, 0)

    def finish(d, carry):
        block = lax.rem(sme + S - d, S)
        for zd in range(1, Z):
            peer = lax.rem(zme + zd, Z)
            k_copy(zd, d, lax.rem(zme + Z - zd, Z), peer, block).wait_recv()
            k_copy(zd, d, zme, peer, block).wait_send()
        if H == 2:
            q_copy(d, 1 - hme, block).wait_recv()
            q_copy(d, hme, block).wait_send()
        return carry

    for d in range(1, S):
        peer = lax.rem(sme + d, S)
        u_copy(d, sme, peer).wait_send()
    for d in range(1, Z):
        w_copy(d, zme, lax.rem(zme + d, Z)).wait_send()
    for c in range(C):
        f_copy(c, core).wait_send()
        if c:
            t_copy(c, sme).wait_send()
    lax.fori_loop(0, S, finish, 0)


def attend_kernel(S, Z, H, per_shard, pat_ref, qu_ref, kv_ref, do_ref, dkv_ref, acc):
    zme = lax.axis_index("zero")
    hme = zme % H
    local = S * per_shard
    total = Z * local
    scale = HEAD ** (-0.5)

    def clear(i, carry):
        acc[i] = jnp.zeros((BLOCK, LANES), F32)
        return carry

    lax.fori_loop(0, total, clear, 0)
    is_q = lax.broadcasted_iota(jnp.int32, (BLOCK, LANES), 1) // HEAD == hme
    is_dq = lax.broadcasted_iota(jnp.int32, (LANES, BLOCK), 0) // HEAD == hme

    def nt(x, y):
        return lax.dot_general(x, y, (((1,), (1,)), ((), ())), preferred_element_type=F32)

    def begin(i):
        r = i % local
        row = (r // per_shard * Z + zme - hme + i // local) * per_shard + r % per_shard
        slots = []
        for j in range(NBK):
            b = pat_ref[row, j]
            shard = b // per_shard
            slots.append(shard % Z * local + shard // Z * per_shard + b % per_shard)
        qu = qu_ref[i]
        none = jnp.zeros_like(qu)
        both = jnp.concatenate([jnp.where(is_q, qu, none), jnp.where(is_q, none, qu)], axis=0)
        keys = jnp.concatenate([kv_ref[s] for s in slots], axis=0)
        return slots, both, keys, nt(keys, both)

    def soften(mixed):
        scores = mixed[:, :BLOCK] * scale
        grad = mixed[:, BLOCK:]
        top = jnp.max(scores, axis=0, keepdims=True)
        exponent = jnp.exp(scores - top)
        inverse = 1.0 / jnp.sum(exponent, axis=0, keepdims=True)
        delta = jnp.sum(exponent * grad, axis=0, keepdims=True) * inverse
        low = (exponent * inverse).astype(BF16)
        sg = (exponent * (inverse * scale) * (grad - delta)).astype(BF16)
        return jnp.concatenate([sg, low], axis=1)

    def end(i, slots, both, keys, pair):
        outs = lax.dot_general(keys, pair, (((0,), (0,)), ((), ())), preferred_element_type=F32)
        do_ref[i] = jnp.where(is_dq, outs[:, :BLOCK], outs[:, BLOCK:]).T.astype(BF16)
        terms = jnp.dot(pair, both, preferred_element_type=F32)
        for j in range(NBK):
            acc[slots[j]] += terms[j * BLOCK : (j + 1) * BLOCK]

    def step(t, carry):
        one, two = 2 * t, 2 * t + 1
        slots_one, both_one, keys_one, mixed_one = begin(one)
        slots_two, both_two, keys_two, mixed_two = begin(two)
        pair_one = soften(mixed_one)
        pair_two = soften(mixed_two)
        end(one, slots_one, both_one, keys_one, pair_one)
        end(two, slots_two, both_two, keys_two, pair_two)
        return carry

    lax.fori_loop(0, H * local // 2, step, 0)

    def store(i, carry):
        dkv_ref[i] = acc[i].astype(BF16)
        return carry

    lax.fori_loop(0, total, store, 0)


def reduce_kernel(
    S, Z, H, do_ref, dkv_ref, tokg_ref, wg_ref, att_ref, tg_ref, wout_ref,
    dbuf, osend, kbuf, grads, wacc, wsend, wbuf, wo, att, part, csend, cbuf, tsend, tbuf,
    ds, dr, os, orr, ks, kr, ws, wr, cs, cr, ts, tr, gs, gr, fs, fr,
):
    sme, zme = lax.axis_index("seq"), lax.axis_index("zero")
    hme = lax.rem(zme, H)
    mate = zme + 1 - 2 * hme
    C = S // 2
    core = lax.rem(sme, 2)
    chip = sme // 2
    twin = sme + 1 - 2 * core
    T = tg_ref.shape[0]
    W = wo.shape[2]
    R = S * T
    hc = H * HEAD

    def rows(i):
        return pl.ds(pl.multiple_of(i * T, T), T)

    def wrows(i):
        return pl.ds(pl.multiple_of(i * W, W), W)

    def speer(d):
        return lax.rem(sme + d, S)

    def sfrom(d):
        return lax.rem(sme + S - d, S)

    def zpeer(d):
        return lax.rem(zme + d, Z)

    def d_copy():
        return remote(do_ref.at[1 - hme], dbuf, ds, dr, (sme, mate))

    def k_copy(d):
        return remote(dkv_ref.at[zpeer(d)], kbuf.at[d - 1], ks.at[d], kr.at[d], (sme, zpeer(d)))

    def there(d):
        return lax.rem(chip + d, C)

    def back(d):
        return lax.rem(chip + C - d, C)

    def o_copy(d, owner):
        return remote(
            osend.at[rows(speer(d))], att.at[owner], os.at[d], orr.at[d], (speer(d), zme)
        )

    def w_copy(d, i):
        return remote(
            wsend.at[i, wrows(zpeer(d))], wbuf.at[d - 1, i], ws.at[d, i], wr.at[d, i],
            (sme, zpeer(d)),
        )

    def c_copy(d):
        return remote(csend.at[d], cbuf.at[d], cs.at[d], cr.at[d], (twin, zme))

    def t_copy(d):
        return remote(
            tsend.at[d - 1], tbuf.at[d - 1], ts.at[d], tr.at[d], (there(d) * 2 + core, zme)
        )

    def span(k):
        return pl.ds(0, 1) if k == 0 else pl.ds(1, wo.shape[1] - 1)

    def g_copy(k, d, owner):
        block = wo.at[sme, span(k)]
        return remote(
            block, wo.at[owner, span(k)], gs.at[k, d], gr.at[k, d], (there(d) * 2 + core, zme)
        )

    def f_copy(k, d, side):
        block = wo.at[back(d) * 2 + core, span(k)]
        return remote(
            block, wo.at[back(d) * 2 + side, span(k)], fs.at[k, d], fr.at[k, d], (twin, zme)
        )

    def weight_part(i):
        part = lax.dot_general(
            tokg_ref[...], grads[i], (((0,), (0,)), ((), ())), preferred_element_type=F32
        )
        wacc[i] = part
        wsend[i] = part.astype(BF16)

    greet(S, Z, sme, zme)
    if H == 2:
        d_copy().start()
    for d in range(1, Z):
        k_copy(d).start()
    half = first_half((R, LANES))
    own = do_ref[hme]
    if H == 2:
        d_copy().wait_recv()
        other = dbuf[...]
        even = jnp.where(hme == 0, own, other)
        odd = jnp.where(hme == 0, other, own)
        grads[0] = jnp.where(half, even, odd)
        osend[...] = turn(jnp.where(half, odd, even))
    else:
        grads[0] = jnp.where(half, own, jnp.zeros_like(own))
        osend[...] = own
    for d in range(1, S):
        o_copy(d, sme).start()
    att[sme] = osend[rows(sme), :]
    weight_part(0)
    for d in range(1, Z):
        w_copy(d, 0).start()
    for d in range(1, Z):
        k_copy(d).wait_recv()
    for h in range(H):
        total = dkv_ref[zme].astype(F32) if h == 0 else None
        for d in range(1, Z):
            if d % H == h:
                term = kbuf[d - 1].astype(F32)
                total = term if total is None else total + term
        grads[1 + lax.rem(hme + h, H)] = total.astype(BF16)
    for h in range(H):
        weight_part(1 + h)
        for d in range(1, Z):
            w_copy(d, 1 + h).start()

    def weight_sum(i):
        for d in range(1, Z):
            w_copy(d, i).wait_recv()
        total = wacc[i, wrows(zme), :]
        for d in range(1, Z):
            total += wbuf[d - 1, i].astype(F32)
        return total

    def share(k):
        for d in range(1, C):
            g_copy(k, d, sme).start()
        f_copy(k, 0, core).start()

    def forward(k):
        for d in range(1, C):
            g_copy(k, d, back(d) * 2 + core).wait_recv()
            f_copy(k, d, core).start()

    wo[sme, 0] = weight_sum(0).astype(BF16)
    share(0)

    def token_part(block):
        total = None
        for i in range(1 + H):
            term = lax.dot_general(
                grads[i, rows(block), :], wg_ref[i], (((1,), (1,)), ((), ())),
                preferred_element_type=F32,
            )
            total = term if total is None else total + term
        return total

    def twin_part(j, carry):
        d = lax.rem(j + 1, C)
        csend[d] = token_part(there(d) * 2 + 1 - core).astype(BF16)
        c_copy(d).start()
        return carry

    lax.fori_loop(0, C, twin_part, 0)

    def own_part(d, carry):
        total = token_part(there(d) * 2 + core)
        c_copy(d).wait_recv()
        tsend[d - 1] = (total + cbuf[d].astype(F32)).astype(BF16)
        t_copy(d).start()
        return carry

    lax.fori_loop(1, C, own_part, 0)
    part[...] = token_part(sme)
    c_copy(0).wait_recv()
    part[...] += cbuf[0].astype(F32)
    forward(0)
    sums = [weight_sum(1 + h) for h in range(H)]
    if H == 2:
        cut = first_half((W, LANES))
        value = pltpu.roll(jnp.where(cut, sums[1], sums[0]), HEAD, 1)
        sums = [jnp.where(cut, sums[0], sums[1]), value]
    for h in range(H):
        wo[sme, 1 + h] = sums[h].astype(BF16)
    share(1)
    for d in range(1, C):
        t_copy(d).wait_recv()
        part[...] += tbuf[d - 1].astype(F32)
    tg_ref[...] = part[...].astype(BF16)
    for d in range(1, S):
        o_copy(d, sfrom(d)).wait_recv()
    for p in range(S):
        block = att[p]
        att_ref[:, p * hc : (p + 1) * hc] = block if H == 2 else block[:, HEAD:]
    forward(1)
    for k in range(2):
        for d in range(C):
            f_copy(k, d, 1 - core).wait_recv()
        for p in range(S):
            for i in range(3) if H == 2 else ():
                if (k == 0) == (i == 0):
                    lo = (i * S + p) * hc
                    wout_ref[:, lo : lo + hc] = wo[p, i]
    if H == 1:
        for p in range(S):
            both = wo[p, 1].astype(F32)
            three = [wo[p, 0].astype(F32)[:, :HEAD], both[:, :HEAD], both[:, HEAD:]]
            for i in range(3):
                lo = (i * S + p) * hc
                wout_ref[:, lo : lo + hc] = three[i].astype(BF16)
    if H == 2:
        d_copy().wait_send()
    for d in range(1, Z):
        k_copy(d).wait_send()
        for i in range(1 + H):
            w_copy(d, i).wait_send()
    for d in range(1, S):
        o_copy(d, sme).wait_send()
    for d in range(C):
        c_copy(d).wait_send()
        for k in range(2):
            f_copy(k, d, core).wait_send()
        if d:
            t_copy(d).wait_send()
            for k in range(2):
                g_copy(k, d, sme).wait_send()


def dma(*shape):
    return pltpu.SemaphoreType.DMA(shape)


def on_device(tokens, projection, pattern, upstream):
    S = lax.axis_size("seq")
    Z = lax.axis_size("zero")
    T, D = tokens.shape
    hc = HEADS // S * HEAD
    W = projection.shape[0]
    R = S * T
    per_shard = T // BLOCK
    H = hc // HEAD
    total = Z * S * per_shard
    shape = jax.ShapeDtypeStruct
    own, up = projection, upstream
    if H == 1:
        own = lax.dynamic_index_in_dim(
            projection.reshape(W, 3, S, hc), lax.axis_index("seq"), axis=2, keepdims=False
        )
        own = own.transpose(1, 0, 2)
        up = upstream.reshape(T, S, hc).transpose(1, 0, 2)
        own = jnp.stack(
            [
                jnp.concatenate([own[0], jnp.zeros_like(own[0])], axis=1),
                jnp.concatenate([own[1], own[2]], axis=1),
            ]
        )
        up = jnp.concatenate([jnp.zeros_like(up), up], axis=2)
    tokg, wg, kv, qu = pl.pallas_call(
        functools.partial(gather_kernel, S, Z, H),
        out_shape=(
            shape((R, D), BF16), shape((1 + H, D, LANES), BF16),
            shape((Z, R, LANES), BF16), shape((H, R, LANES), BF16),
        ),
        in_specs=[VMEM, pl.BlockSpec(memory_space=pl.ANY) if H == 2 else VMEM, VMEM],
        out_specs=(VMEM,) * 4,
        scratch_shapes=[
            pltpu.VMEM((3, W, LANES), BF16),
            dma(3),
            pltpu.VMEM((1 + H, W, LANES), BF16),
            pltpu.VMEM((H, R, LANES), BF16),
            pltpu.VMEM((H, R, LANES), BF16),
            pltpu.VMEM((R, LANES), BF16),
            dma(S), dma(S), dma(Z), dma(Z), dma(S), dma(S), dma(Z, S), dma(Z, S), dma(S), dma(S),
        ],
        compiler_params=pltpu.CompilerParams(
            collective_id=0, has_side_effects=True, vmem_limit_bytes=LIMIT
        ),
        name="gather",
    )(tokens, own, up)
    do, dkv = pl.pallas_call(
        functools.partial(attend_kernel, S, Z, H, per_shard),
        out_shape=(
            shape((H * S * per_shard, BLOCK, LANES), BF16), shape((total, BLOCK, LANES), BF16),
        ),
        in_specs=[SMEM] + [VMEM] * 2,
        out_specs=(VMEM,) * 2,
        scratch_shapes=[pltpu.VMEM((total, BLOCK, LANES), F32)],
        compiler_params=pltpu.CompilerParams(vmem_limit_bytes=LIMIT),
        name="attend",
    )(
        pattern,
        qu.reshape(H * S * per_shard, BLOCK, LANES),
        kv.reshape(total, BLOCK, LANES),
    )
    att, tg, wo = pl.pallas_call(
        functools.partial(reduce_kernel, S, Z, H),
        out_shape=(
            shape((T, S * hc), BF16), shape((T, D), BF16), shape((W, 3 * S * hc), BF16),
        ),
        in_specs=[VMEM] * 4,
        out_specs=(VMEM,) * 3,
        scratch_shapes=[
            pltpu.VMEM((R, LANES), BF16),
            pltpu.VMEM((R, LANES), BF16),
            pltpu.VMEM((Z - 1, R, LANES), BF16),
            pltpu.VMEM((1 + H, R, LANES), BF16),
            pltpu.VMEM((1 + H, D, LANES), F32),
            pltpu.VMEM((1 + H, D, LANES), BF16),
            pltpu.VMEM((Z - 1, 1 + H, W, LANES), BF16),
            pltpu.VMEM((S, 1 + H, W, LANES), BF16),
            pltpu.VMEM((S, T, LANES), BF16),
            pltpu.VMEM((T, D), F32),
            pltpu.VMEM((S // 2, T, D), BF16),
            pltpu.VMEM((S // 2, T, D), BF16),
            pltpu.VMEM((S // 2 - 1, T, D), BF16),
            pltpu.VMEM((S // 2 - 1, T, D), BF16),
            pltpu.SemaphoreType.DMA, pltpu.SemaphoreType.DMA,
            dma(S), dma(S), dma(Z), dma(Z), dma(Z, 1 + H), dma(Z, 1 + H),
            dma(S // 2), dma(S // 2), dma(S // 2), dma(S // 2),
            dma(2, S // 2), dma(2, S // 2), dma(2, S // 2), dma(2, S // 2),
        ],
        compiler_params=pltpu.CompilerParams(
            collective_id=1, has_side_effects=True, vmem_limit_bytes=LIMIT
        ),
        name="reduce",
    )(do.reshape(H, R, LANES), dkv.reshape(Z, R, LANES), tokg, wg)
    return (att, tg, wo.astype(F32))


def solution(mesh):
    return jax.shard_map(
        on_device,
        mesh=mesh,
        in_specs=(P(("seq", "zero"), None), P("zero", None), P(), P(("seq", "zero"), None)),
        out_specs=(P(("seq", "zero"), None), P(("seq", "zero"), None), P("zero", None)),
        check_vma=False,
    )
```
